512 devices in a mesh: tile: 32 (over x, y, core), slide: 16 (over z).
Axes of the slice: x: 4, y: 4, z: 16, core: 2. Of those that a mesh axis runs over, the one named last changes fastest.
Arguments:
- tile_maps: bfloat16 [8192, 8, 8, 768], P(('tile', 'slide')), may hold values from -6 to 6
- dw_kernel: bfloat16 [49, 768], replicated, may hold values from -0.875 to 0.875
- conv_bias: float32 [768], replicated, may hold values from -0.9 to 0.9
- norm_gain: float32 [768], replicated, may hold values from 0.1 to 1.9
- w_in: bfloat16 [768, 768], replicated, may hold values from -1.75 to 1.75
- w_qkv: bfloat16 [768, 2304], P(None, 'slide'), may hold values from -0.21875 to 0.21875
- seg_len: int32 [16], replicated, may hold values from 4 to 16, as said below
- dilation: int32 [16], replicated, may hold values from 1 to 4, as said below
- tile_slot: int32 [8192], P(('tile', 'slide')), may hold values from 0 to 255, as said below
- slide_lengths: int32 [512, 2], P(('tile', 'slide')), may hold values from 0 to 16, as said below
- cotangent: bfloat16 [8192, 768], P(('tile', 'slide')), may hold values from -0.119628906 to 0.119628906
Outputs:
- attn_out: bfloat16 [8192, 768], P(('tile', 'slide'))
- grad_kernel: float32 [49, 768], replicated
- grad_norm: float32 [2, 768], replicated
The draws below stay inside these ranges and needn't reach their ends.
Inputs may be any that keep to these rules, and one draw needn't show every extreme that they name: `tile_slot`: within each group, the tiles' slots are each of 0 to 255 once; slot // 16 is the owner along slide; at most 3 tiles of one device go to one owner, and that many do in every draw. `slide_lengths`: each owner's two lengths add up to 16. `seg_len`: each is 4, 8 or 16, and each of the three occurs. `dilation`: each is 1, 2 or 4, and each of the three occurs.
All inputs are finite; a program needn't handle non-finite values.
Results may differ from the reference program's by a relative error of at most 0.024.
Values may be sent and summed in bfloat16 or wider, within the bound.
A program may use at most 64 MiB of HBM per device.

```python
import jax
import jax.numpy as jnp
from jax import lax

C = 768
D = 768
HEADS = 16
SIDE = 8
TOK_DEV = 16
KK = 49
SEND = 3
TILES = 8192
N_TILE = 32
N_SLIDE = 16


def draw_tile_slot(key, part):
    key = jax.random.fold_in(key, 11)
    quota = [SEND] * (TOK_DEV // SEND)
    if TOK_DEV % SEND:
        quota = quota + [TOK_DEV % SEND]
    quota = quota + [0] * (N_SLIDE - len(quota))
    base = jnp.array(quota, jnp.int32)

    def one_group(group_key):
        spread_key, order_key = jax.random.split(group_key)
        spread = base[jax.random.permutation(spread_key, N_SLIDE)]
        source = jnp.arange(N_SLIDE, dtype=jnp.int32)
        counts = spread[(source[None, :] - source[:, None]) % N_SLIDE]
        before = jnp.cumsum(counts, axis=0) - counts
        upto = jnp.cumsum(counts, axis=1)
        ranks = jnp.arange(TOK_DEV, dtype=jnp.int32)
        owner = jnp.sum((ranks[None, :, None] >= upto[:, None, :]).astype(jnp.int32), axis=2)
        start = jnp.take_along_axis(upto - counts, owner, axis=1)
        offset = jnp.take_along_axis(before, owner, axis=1)
        slots = owner * TOK_DEV + offset + ranks[None, :] - start
        order = jax.vmap(lambda each_key: jax.random.permutation(each_key, TOK_DEV))(jax.random.split(order_key, N_SLIDE))
        return jnp.take_along_axis(slots, order, axis=1).reshape(-1)
    return jax.vmap(one_group)(jax.random.split(key, N_TILE)).reshape(-1).astype(jnp.int32)


def draw_slide_lengths(key, part):
    key = jax.random.fold_in(key, 13)
    boundary_key, within_key, chosen_key = jax.random.split(key, 3)
    blocks = N_TILE * N_SLIDE
    boundary = jax.random.randint(boundary_key, (blocks,), 1, TOK_DEV)
    within = jax.random.randint(within_key, (blocks,), 0, 8) > 0
    forced = jnp.arange(blocks, dtype=jnp.int32) == jax.random.randint(chosen_key, (), 0, blocks)
    leading = jnp.where(within | forced, TOK_DEV, boundary)
    return jnp.stack([leading, TOK_DEV - leading], axis=1).astype(jnp.int32)


def head_levels(key):
    level_key, order_key = jax.random.split(key)
    levels = jax.random.randint(level_key, (HEADS,), 0, 3)
    chosen = jax.random.permutation(order_key, HEADS)[:3]
    return levels.at[chosen].set(jnp.arange(3, dtype=jnp.int32))


def ladder_factor(levels):
    return jnp.where(levels == 0, 1, jnp.where(levels == 1, 2, 4))


def draw_seg_len(key, part):
    key = jax.random.fold_in(key, 17)
    levels = head_levels(key)
    return (TOK_DEV // 4 * ladder_factor(levels)).astype(jnp.int32)


def draw_dilation(key, part):
    key = jax.random.fold_in(key, 19)
    levels = head_levels(key)
    return ladder_factor(levels).astype(jnp.int32)


def block_scale(key, dims, shards, least, high):
    def one(axis_at, parts):
        heights = jax.random.uniform(jax.random.fold_in(jax.random.fold_in(key, 6), axis_at), (parts,), jnp.float32, least / len(shards), high / len(shards))
        return jnp.repeat(jnp.exp(heights), dims[axis_at] // parts).reshape((-1,) + (1,) * (len(dims) - axis_at - 1))

    loudness = one(*shards[0])
    for cut in shards[1:]:
        loudness = loudness * one(*cut)
    return loudness


def noise(key, shape, deviation, reach, shards=(), kind=jnp.bfloat16):
    values = jax.random.normal(key, shape, jnp.float32) * deviation
    if len(shards) > 0:
        values = block_scale(key, shape, shards, -0.22, 0.18) * values
    return jnp.clip(values, min=-reach, max=reach).astype(kind)


def setup_inputs(seed: int = 0) -> dict:
    splits = jax.random.split(jax.random.key(seed), 12)
    return {
        "tile_maps": noise(splits[0], (TILES, SIDE, SIDE, C), 1.0, 6.0, ((0, 512),)),
        "dw_kernel": noise(splits[1], (KK, C), KK ** -0.5, 0.875),
        "conv_bias": noise(splits[2], (C,), 0.15, 0.9, (), jnp.float32),
        "norm_gain": jnp.clip(1.0 + 0.18 * jax.random.normal(splits[3], (C,), jnp.float32), 0.1, 1.9),
        "w_in": noise(splits[4], (C, D), (C // 64) ** -0.5, 1.75),
        "w_qkv": noise(splits[5], (D, 3 * D), D ** -0.5, 0.21875, ((1, 16),)),
        "seg_len": draw_seg_len(jax.random.fold_in(splits[11], 71), 0),
        "dilation": draw_dilation(jax.random.fold_in(splits[11], 71), 0),
        "tile_slot": draw_tile_slot(jax.random.fold_in(splits[11], 71), 0),
        "slide_lengths": draw_slide_lengths(jax.random.fold_in(splits[11], 71), 0),
        "cotangent": noise(splits[10], (TILES, D), 0.02, 0.119628906, ((0, 512),)),
    }


norm_eps = 1e-06

def encode(tile_maps, dw_kernel, conv_bias, norm_gain, w_in):
    channels = tile_maps.shape[3]
    conv = lax.conv_general_dilated(tile_maps.astype(jnp.float32), dw_kernel.astype(jnp.float32).reshape(7, 7, 1, channels), (1, 1), ((3, 3), (3, 3)), dimension_numbers=('NHWC', 'HWIO', 'NHWC'), feature_group_count=channels, precision=lax.Precision.HIGHEST) + conv_bias
    centered = conv - lax.optimization_barrier(jnp.mean(conv, axis=3, keepdims=True))
    inverse_std = lax.rsqrt(lax.optimization_barrier(jnp.mean(centered * centered, axis=3, keepdims=True)) + norm_eps)
    normed = centered * inverse_std
    pooled = lax.optimization_barrier(jnp.mean(normed * norm_gain, axis=(1, 2))).astype(jnp.bfloat16)
    embed = jnp.dot(pooled, w_in, preferred_element_type=jnp.float32).astype(jnp.bfloat16)
    return (embed, normed, inverse_std)

def tile_grads(tile_maps, normed, inverse_std, norm_gain, w_in, dembed):
    side = tile_maps.shape[1]
    area = side * side
    dpool = lax.dot_general(dembed, w_in, (((1,), (1,)), ((), ())), preferred_element_type=jnp.float32)
    dnormed = dpool[:, None, None, :] * (norm_gain / area)
    inner = lax.optimization_barrier(jnp.mean(dnormed, axis=3, keepdims=True))
    along = lax.optimization_barrier(jnp.mean(dnormed * normed, axis=3, keepdims=True))
    dconv = inverse_std * (dnormed - inner - normed * along)
    padded = jnp.pad(tile_maps, ((0, 0), (3, 3), (3, 3), (0, 0)))
    taps = [lax.optimization_barrier(jnp.sum(padded[:, row_off:row_off + side, col_off:col_off + side, :].astype(jnp.float32) * dconv, axis=(0, 1, 2))) for row_off in range(7) for col_off in range(7)]
    grad_bias = lax.optimization_barrier(jnp.sum(dconv, axis=(0, 1, 2)))
    grad_gain = lax.optimization_barrier(jnp.sum(dpool * lax.optimization_barrier(jnp.sum(normed, axis=(1, 2))), axis=0)) / area
    return (jnp.stack(taps), jnp.stack([grad_bias, grad_gain]))

def slot_layout(lengths, capacity):
    owners, slides = lengths.shape
    ends = jnp.cumsum(lengths, axis=1).astype(jnp.int32)
    index = jnp.arange(capacity, dtype=jnp.int32)
    label = lax.optimization_barrier(jnp.sum((index[None, :, None] >= ends[:, None, :]).astype(jnp.int32), axis=2)).astype(jnp.int32)
    match = label[:, :, None] == jnp.arange(slides, dtype=jnp.int32)[None, None, :]
    begin = lax.optimization_barrier(jnp.sum(jnp.where(match, (ends - lengths)[:, None, :], 0), axis=2)).astype(jnp.int32)
    position = index[None, :] - begin
    slide_id = jnp.arange(owners, dtype=jnp.int32)[:, None] * slides + label
    return (slide_id.reshape(-1), position.reshape(-1))

def head_mask(slide_id, position, seg_len, dilation):
    same = slide_id[:, None] == slide_id[None, :]
    segment = position[None, :] // seg_len[:, None]
    residue = position[None, :] % dilation[:, None]
    return same[None] & (segment[:, :, None] == segment[:, None, :]) & (residue[:, :, None] == residue[:, None, :])

def head_pass(qkv, upstream, allowed, scale):
    queries = qkv[:, :, 0].astype(jnp.float32)
    key_rows = qkv[:, :, 1].astype(jnp.float32)
    value_rows = qkv[:, :, 2].astype(jnp.float32)
    scores = jnp.einsum('ihd,jhd->hij', queries, key_rows) * scale
    masked = jnp.where(allowed, scores, -1e+30)
    top = lax.optimization_barrier(jnp.max(masked, axis=2, keepdims=True))
    expo = jnp.where(allowed, jnp.exp(masked - top), 0.0)
    prob = expo / lax.optimization_barrier(jnp.sum(expo, axis=2, keepdims=True))
    weights = lax.optimization_barrier(prob.astype(jnp.bfloat16)).astype(jnp.float32)
    mixed = jnp.einsum('hij,jhd->ihd', weights, value_rows).astype(jnp.bfloat16)
    grads = upstream.astype(jnp.float32)
    dprob = jnp.einsum('ihd,jhd->hij', grads, value_rows)
    dvalue = jnp.einsum('hij,ihd->jhd', weights, grads)
    dscore = prob * (dprob - lax.optimization_barrier(jnp.sum(prob * dprob, axis=2, keepdims=True))) * scale
    dscore = lax.optimization_barrier(dscore.astype(jnp.bfloat16)).astype(jnp.float32)
    dquery = jnp.einsum('hij,jhd->ihd', dscore, key_rows)
    dkey = jnp.einsum('hij,ihd->jhd', dscore, queries)
    dqkv = jnp.stack([dquery, dkey, dvalue], axis=2).astype(jnp.bfloat16)
    return (mixed, dqkv)

def reference(tile_maps, dw_kernel, conv_bias, norm_gain, w_in, w_qkv, seg_len, dilation, tile_slot, slide_lengths, cotangent):
    width = w_in.shape[1]
    heads = seg_len.shape[0]
    head_size = width // heads
    scale = head_size ** (-0.5)
    group = N_SLIDE * TOK_DEV

    def one_group(inputs):
        maps, slots, lengths, upstream = inputs
        embed, normed, inverse_std = encode(maps, dw_kernel, conv_bias, norm_gain, w_in)
        layout = jnp.zeros((group, width), jnp.bfloat16).at[slots].set(embed)

        def one_owner(block_inputs):
            block, lengths_one, block_grads = block_inputs
            slide_id, position = slot_layout(lengths_one[None, :], TOK_DEV)
            allowed = head_mask(slide_id, position, seg_len, dilation)
            qkv = jnp.dot(block, w_qkv, preferred_element_type=jnp.float32).astype(jnp.bfloat16).reshape(TOK_DEV, heads, 3, head_size)
            mixed, dqkv = head_pass(qkv, block_grads.reshape(TOK_DEV, heads, head_size), allowed, scale)
            grouped = jnp.einsum('rgk,dgk->grd', dqkv.reshape(TOK_DEV, N_SLIDE, -1).astype(jnp.float32), w_qkv.reshape(width, N_SLIDE, -1).astype(jnp.float32))
            rounded = lax.optimization_barrier(grouped.astype(jnp.bfloat16)).astype(jnp.float32)
            dblock = lax.optimization_barrier(jnp.sum(rounded, axis=0)).astype(jnp.bfloat16)
            return (mixed.reshape(TOK_DEV, width), dblock)
        mixed, dlayout = lax.map(one_owner, (layout.reshape(N_SLIDE, TOK_DEV, width), lengths, upstream.reshape(N_SLIDE, TOK_DEV, width)))
        dembed = dlayout.reshape(group, width)[slots]
        kernel_part, norm_part = tile_grads(maps, normed, inverse_std, norm_gain, w_in, dembed)
        return (mixed.reshape(group, width), kernel_part, norm_part)
    mixed, kernel_parts, norm_parts = lax.map(one_group, (tile_maps.reshape(N_TILE, group, SIDE, SIDE, -1), tile_slot.reshape(N_TILE, group), slide_lengths.reshape(N_TILE, N_SLIDE, -1), cotangent.reshape(N_TILE, group, width)))
    return (mixed.reshape(-1, width), lax.optimization_barrier(jnp.sum(kernel_parts, axis=0)), lax.optimization_barrier(jnp.sum(norm_parts, axis=0)))
```

```python
import jax
import jax.numpy as jnp
from jax import lax
from jax.experimental import pallas as pl
from jax.experimental.pallas import tpu as pltpu
from jax.sharding import PartitionSpec as P

NORM_EPS = 1e-06
MESH = pl.DeviceIdType.MESH
BF = jnp.bfloat16
F32 = jnp.float32

SIDE = 8
AREA = SIDE * SIDE
REACH = 3
TAPS = 7
ROWS = 16
C = 768
LANE = 128
CHUNKS = C // LANE
HEADS = 16
HEAD = 48
SLIDES = 16
PLANE = 32
QUOTA = 3
PACK = 32
HALF = C // 2
UNITS = 24
SUM_ROWS = 64


def iota(shape, dim):
    return lax.broadcasted_iota(jnp.int32, shape, dim)


def dot(left, right):
    return jnp.dot(left, right, preferred_element_type=F32)


def dot_last(left, right):
    return lax.dot_general(left, right, (((1,), (1,)), ((), ())), preferred_element_type=F32)


def dot_first(left, right):
    return lax.dot_general(left, right, (((0,), (0,)), ((), ())), preferred_element_type=F32)


def spread(block):
    return jnp.concatenate([block[:, k * LANE : (k + 1) * LANE] for k in range(CHUNKS)], axis=0)


def gather_chunks(stack):
    return jnp.concatenate([stack[k * ROWS : (k + 1) * ROWS] for k in range(CHUNKS)], axis=1)


def row_span(offset):
    return max(0, -offset), min(SIDE, SIDE - offset)


def transpose_maps(maps_ref, xt_ref):
    row, col = iota((128, 128), 0), iota((128, 128), 1)
    perm = ((row >> 4) == (col & 7)) & ((row & 15) == (col >> 3))
    perm = perm.astype(F32).astype(BF)
    for r in range(SIDE):
        part = maps_ref[:, r].astype(F32).reshape(128, C).astype(BF)
        xt_ref[r] = dot(perm, part).astype(BF).reshape(SIDE, ROWS, C)


def spread_taps(dw_ref, wb_ref):
    taps = dw_ref[...].astype(F32)
    for tap in range(TAPS * TAPS):
        wb_ref[tap] = jnp.broadcast_to(taps[tap : tap + 1], (ROWS, C)).astype(BF)


def conv_chunk(chunk, xt_ref, wb_ref, bias_ref, cv_ref):
    lanes = pl.ds(pl.multiple_of(chunk * LANE, LANE), LANE)
    bias = jnp.broadcast_to(bias_ref[:, lanes], (ROWS, LANE))
    for i in range(SIDE):
        total = [bias] * SIDE
        for r in range(TAPS):
            src = i + r - REACH
            if not 0 <= src < SIDE:
                continue
            cells = [xt_ref[src, j, :, lanes] for j in range(SIDE)]
            taps = [wb_ref[r * TAPS + s, :, lanes] for s in range(TAPS)]
            for j in range(SIDE):
                acc = None
                for s in range(TAPS):
                    at = j + s - REACH
                    if 0 <= at < SIDE:
                        term = cells[at] * taps[s]
                        acc = term if acc is None else acc + term
                total[j] = total[j] + acc.astype(F32)
        for j in range(SIDE):
            cv_ref[i * SIDE + j, :, lanes] = total[j]


def normalise(cv_ref, nrm_ref, inv_ref):
    def step(p, total):
        conv = cv_ref[p]
        centered = conv - jnp.mean(conv, axis=1, keepdims=True)
        inv = lax.rsqrt(jnp.mean(centered * centered, axis=1, keepdims=True) + NORM_EPS)
        normed = centered * inv
        nrm_ref[p] = normed.astype(BF)
        inv_ref[p] = jnp.broadcast_to(inv, (ROWS, LANE))
        return total + normed

    return lax.fori_loop(0, AREA, step, jnp.zeros((ROWS, C), F32), unroll=2)


def forward_kernel(
    maps_ref, dw_ref, bias_ref, gain_ref, win_ref,
    xt_ref, nrm_ref, inv_ref, sum_ref, embed_ref,
    wb_ref, cv_ref,
):
    transpose_maps(maps_ref, xt_ref)
    spread_taps(dw_ref, wb_ref)

    @pl.loop(0, CHUNKS)
    def _(chunk):
        conv_chunk(chunk, xt_ref, wb_ref, bias_ref, cv_ref)

    total = normalise(cv_ref, nrm_ref, inv_ref)
    sum_ref[...] = total
    pooled = (total * gain_ref[...] * (1.0 / AREA)).astype(BF)
    embed_ref[...] = dot(pooled, win_ref[...]).astype(BF)


def send_rows(slot_ref):
    lane = iota((1, 112), 1)
    tile, chunk = lane & 15, lane >> 4
    owner = jnp.zeros((1, 112), jnp.int32)
    for t in range(ROWS):
        owner = jnp.where(tile == t, slot_ref[t] >> 4, owner)
    rank = jnp.zeros((1, 112), jnp.int32)
    for t in range(ROWS):
        rank = rank + jnp.where((owner == (slot_ref[t] >> 4)) & (tile > t), 1, 0)
    want = owner * PACK + chunk * QUOTA + rank
    select = (iota((SLIDES * PACK, 112), 0) == want).astype(F32).astype(BF)
    sub = iota((ROWS, LANE), 0)
    slots = jnp.zeros((ROWS, LANE), jnp.int32)
    for t in range(ROWS):
        slots = jnp.where(sub == t, (slot_ref[t] & 15) + 1, slots)
    return select, slots.astype(F32).astype(BF)


def slot_spread():
    size = SLIDES * PACK
    row, col = iota((size, size), 0), iota((size, size), 1)
    inside = row & (PACK - 1)
    quota = inside
    for k in range(1, PACK // QUOTA + 1):
        quota = jnp.where(inside >= k * QUOTA, inside - k * QUOTA, quota)
    return (col == (row - inside + CHUNKS * QUOTA + quota)).astype(F32).astype(BF)


def place_rows(spread_slots, arrived):
    size = SLIDES * PACK
    slot = dot(spread_slots, arrived)[:, : CHUNKS * ROWS]
    inside = iota((size, CHUNKS * ROWS), 0) & (PACK - 1)
    lane = iota((size, CHUNKS * ROWS), 1)
    first = (lane >> 4) * QUOTA
    want = ((lane & 15) + 1).astype(F32)
    hit = (inside >= first) & (inside < first + QUOTA) & (slot == want)
    return hit.astype(F32).astype(BF)


def head_mask():
    row, lane = iota((HEADS * ROWS, C), 0), iota((HEADS * ROWS, C), 1)
    low = (row >> 4) * HEAD
    return ((lane >= low) & (lane < low + HEAD)).astype(F32).astype(BF)


def allowed_pairs(seg_ref, dil_ref, len_ref):
    left, right = iota((ROWS, ROWS), 0), iota((ROWS, ROWS), 1)
    cut = len_ref[0, 0]
    run_left, run_right = left >= cut, right >= cut
    pos_left = jnp.where(run_left, left - cut, left)
    pos_right = jnp.where(run_right, right - cut, right)
    apart = pos_left ^ pos_right
    apart = jnp.where(run_left != run_right, apart | 256, apart)
    parts = []
    for h in range(HEADS):
        parts.append(apart & (~(seg_ref[h] - 1) | (dil_ref[h] - 1)))
    return jnp.concatenate(parts, axis=0) == 0


def attention(block, w3_ref, cot_ref, attn_ref, mask, allowed):
    scale = HEAD ** (-0.5)
    weights = [w3_ref[part].reshape(C, C) for part in range(3)]
    query, key, value = [dot_last(block, each).astype(BF) for each in weights]
    many_query = jnp.concatenate([query] * HEADS, axis=0) * mask
    many_grad = jnp.concatenate([cot_ref[...]] * HEADS, axis=0) * mask
    scores = dot_last(many_query, key) * scale
    masked = jnp.where(allowed, scores, -1e30)
    top = jnp.max(masked, axis=1, keepdims=True)
    expo = jnp.where(allowed, jnp.exp(masked - top), 0.0)
    prob = expo / jnp.sum(expo, axis=1, keepdims=True)
    prob_bf = prob.astype(BF)
    mask_f = mask.astype(F32)

    def own_head(full):
        return jnp.sum((full * mask_f).reshape(HEADS, ROWS, C), axis=0)

    attn_ref[...] = own_head(dot(prob_bf, value)).astype(BF)
    dprob = dot_last(many_grad, value)
    dscore = (prob * (dprob - jnp.sum(prob * dprob, axis=1, keepdims=True)) * scale).astype(BF)
    dquery = own_head(dot(dscore, key)).astype(BF)
    dkey = dot_first(dscore, many_query).astype(BF)
    dvalue = dot_first(prob_bf, many_grad).astype(BF)
    total = dot(dquery, weights[0]) + dot(dkey, weights[1]) + dot(dvalue, weights[2])
    return total.astype(BF)


def shift(index, by, size):
    return lax.rem(index + by + size, size)


def core_of(tile):
    return lax.rem(tile, 2)


class Ring:
    def __init__(self, w3_ref, sems):
        self.w3_ref = w3_ref
        self.right, self.left, self.core = sems[0:2], sems[2:4], sems[4:6]
        tile = lax.axis_index("tile")
        self.me = lax.axis_index("slide")
        self.lanes = pl.ds(pl.multiple_of(core_of(tile) * HALF, HALF), HALF)
        self.other = tile + 1 - 2 * core_of(tile)

    def copy(self, head, send_sem, recv_sem, device):
        block = self.w3_ref.at[:, head, :, self.lanes]
        return pltpu.make_async_remote_copy(
            block, block, send_sem, recv_sem, device_id=device, device_id_type=MESH)

    def to_right(self, s):
        return self.copy(
            shift(self.me, -s, SLIDES), self.right[0].at[s], self.right[1].at[s],
            {"slide": shift(self.me, 1, SLIDES)})

    def to_left(self, s):
        return self.copy(
            shift(self.me, s, SLIDES), self.left[0].at[s], self.left[1].at[s],
            {"slide": shift(self.me, -1, SLIDES)})

    def left_to_core(self, s):
        return self.copy(
            shift(self.me, -s, SLIDES), self.core[0].at[0, s], self.core[1].at[0, s],
            {"tile": self.other})

    def right_to_core(self, s):
        return self.copy(
            shift(self.me, s, SLIDES), self.core[0].at[1, s], self.core[1].at[1, s],
            {"tile": self.other})


RIGHT_STEPS = SLIDES // 2
LEFT_STEPS = SLIDES // 2 - 1


def ring_start(wq_ref, w3_ref, ring):
    w3_ref[:, ring.me] = wq_ref[...].reshape(3, HEAD, C)
    ring.to_right(0).start()
    ring.to_left(0).start()


def ring_step(ring, s):
    ring.to_right(s - 1).wait_recv()
    if s < RIGHT_STEPS:
        ring.to_right(s).start()
    ring.left_to_core(s).start()
    if s <= LEFT_STEPS:
        ring.to_left(s - 1).wait_recv()
        if s < LEFT_STEPS:
            ring.to_left(s).start()
        ring.right_to_core(s).start()


def ring_end(ring):
    for s in range(RIGHT_STEPS + 1):
        if s >= 1:
            ring.left_to_core(s).wait()
        if 1 <= s <= LEFT_STEPS:
            ring.right_to_core(s).wait()
        if s < RIGHT_STEPS:
            ring.to_right(s).wait_send()
        if s < LEFT_STEPS:
            ring.to_left(s).wait_send()


def exchange_start(out_ref, in_ref, send_sem, recv_sem):
    me = lax.axis_index("slide")
    in_ref[me] = out_ref[me]

    @pl.loop(1, SLIDES)
    def _(j):
        peer = shift(me, j, SLIDES)
        pltpu.make_async_remote_copy(
            out_ref.at[peer], in_ref.at[me], send_sem, recv_sem,
            device_id={"slide": peer}, device_id_type=MESH).start()


def exchange_wait(out_ref, in_ref, send_sem, recv_sem):
    some = pl.ds(0, SLIDES - 1)
    pltpu.make_async_copy(in_ref.at[some], in_ref.at[some], recv_sem).wait()
    pltpu.make_async_copy(out_ref.at[some], out_ref.at[some], send_sem).wait()


def greet(with_plane):
    tile, me = lax.axis_index("tile"), lax.axis_index("slide")
    barrier = pltpu.get_barrier_semaphore()

    @pl.loop(1, SLIDES)
    def _(j):
        pl.semaphore_signal(
            barrier, inc=1, device_id={"slide": shift(me, j, SLIDES)}, device_id_type=MESH)

    count = SLIDES - 1
    if with_plane:

        @pl.loop(1, PLANE)
        def _(j):
            pl.semaphore_signal(
                barrier, inc=1, device_id={"tile": shift(tile, j, PLANE)}, device_id_type=MESH)

        count += PLANE - 1
    else:
        pl.semaphore_signal(
            barrier, inc=1, device_id={"tile": tile + 1 - 2 * core_of(tile)}, device_id_type=MESH)
        count += 1
    pl.semaphore_wait(barrier, count)


def owner_kernel(
    embed_ref, win_ref, wq_ref, seg_ref, dil_ref, slot_ref, len_ref, cot_ref,
    attn_ref, dpool_ref,
    w3_ref, out_ref, in_ref, back_out_ref, back_in_ref,
    right_send, right_recv, left_send, left_recv, core_send, core_recv, route_sems,
):
    sems = (right_send, right_recv, left_send, left_recv, core_send, core_recv)
    greet(False)
    ring = Ring(w3_ref, sems)
    ring_start(wq_ref, w3_ref, ring)
    select, slots = send_rows(slot_ref)
    packed = jnp.concatenate([spread(embed_ref[...]), slots], axis=0)
    out_ref[...] = dot(select, packed).astype(BF).reshape(SLIDES, PACK, LANE)
    exchange_start(out_ref, in_ref, route_sems.at[0], route_sems.at[1])
    spread_slots, mask = slot_spread(), head_mask()
    allowed = allowed_pairs(seg_ref, dil_ref, len_ref)
    for s in range(1, RIGHT_STEPS + 1):
        ring_step(ring, s)
    exchange_wait(out_ref, in_ref, route_sems.at[0], route_sems.at[1])
    arrived = in_ref[...].reshape(SLIDES * PACK, LANE)
    place = place_rows(spread_slots, arrived)
    block = gather_chunks(dot_first(place, arrived).astype(BF))
    ring_end(ring)
    dblock = attention(block, w3_ref, cot_ref, attn_ref, mask, allowed)
    back_out_ref[...] = dot(place, spread(dblock)).astype(BF).reshape(SLIDES, PACK, LANE)
    exchange_start(back_out_ref, back_in_ref, route_sems.at[2], route_sems.at[3])
    exchange_wait(back_out_ref, back_in_ref, route_sems.at[2], route_sems.at[3])
    returned = back_in_ref[...].reshape(SLIDES * PACK, LANE)
    dembed = gather_chunks(dot_first(select[:, : CHUNKS * ROWS], returned).astype(BF))
    dpool_ref[...] = dot_last(dembed, win_ref[...])


def conv_grads(dpool, gain_ref, nrm_ref, inv_ref, dc_ref):
    grad = dpool * (gain_ref[...] * (1.0 / AREA))
    level = grad - jnp.mean(grad, axis=1, keepdims=True)

    def step(p, total):
        normed = nrm_ref[p].astype(F32)
        along = jnp.mean(grad * normed, axis=1, keepdims=True)
        inv = inv_ref[p][:, :1]
        dconv = inv * (level - normed * along)
        dc_ref[p] = dconv.astype(BF)
        return total + dconv

    return lax.fori_loop(0, AREA, step, jnp.zeros((ROWS, C), F32), unroll=2)


def tap_grads(chunk, xt_ref, dc_ref, part_ref):
    lanes = pl.ds(pl.multiple_of(chunk * LANE, LANE), LANE)
    for r in range(TAPS):
        total = [jnp.zeros((ROWS, LANE), F32)] * TAPS
        for i in range(*row_span(r - REACH)):
            cells = [xt_ref[i + r - REACH, j, :, lanes] for j in range(SIDE)]
            grads = [dc_ref[i * SIDE + j, :, lanes] for j in range(SIDE)]
            for s in range(TAPS):
                acc = None
                for j in range(*row_span(s - REACH)):
                    term = cells[j + s - REACH] * grads[j]
                    acc = term if acc is None else acc + term
                total[s] = total[s] + acc.astype(F32)
        for s in range(TAPS):
            tap = r * TAPS + s
            part_ref[tap : tap + 1, lanes] = jnp.sum(total[s], axis=0, keepdims=True)


def backward_kernel(dpool_ref, gain_ref, xt_ref, nrm_ref, inv_ref, sum_ref, part_ref, dc_ref):
    dpool = dpool_ref[...]
    bias_grad = conv_grads(dpool, gain_ref, nrm_ref, inv_ref, dc_ref)
    part_ref[...] = jnp.zeros(part_ref.shape, F32)
    part_ref[49:50] = jnp.sum(bias_grad, axis=0, keepdims=True)
    part_ref[50:51] = jnp.sum(dpool * sum_ref[...], axis=0, keepdims=True) * (1.0 / AREA)

    @pl.loop(0, CHUNKS)
    def _(chunk):
        tap_grads(chunk, xt_ref, dc_ref, part_ref)


def unit_at(ref, unit):
    rows = pl.ds(pl.multiple_of((unit & 3) * 16, 16), 16)
    lanes = pl.ds(pl.multiple_of((unit >> 2) * LANE, LANE), LANE)
    return ref.at[rows, lanes]


def owner_of(unit):
    return unit + unit // 3


def reduce_all(flat_ref, near_ref, far_ref, res_ref, far_out_ref, sems):
    tile, me = lax.axis_index("tile"), lax.axis_index("slide")
    owner = lax.rem(tile, 4) != 3
    unit = jnp.minimum((tile // 4) * 3 + lax.rem(tile, 4), UNITS - 1)

    @pl.loop(0, UNITS)
    def _(j):
        peer = owner_of(j)

        @pl.when(peer != tile)
        def _():
            pltpu.make_async_remote_copy(
                unit_at(flat_ref, j), near_ref.at[tile], sems.at[0], sems.at[1],
                device_id={"tile": peer}, device_id_type=MESH).start()

    def wait_units(ref, count, sem):
        some = pl.ds(0, count)
        pltpu.make_async_copy(ref.at[some], ref.at[some], sem).wait()

    @pl.when(owner)
    def _():
        near_ref[tile] = unit_at(flat_ref, unit)[...]
        wait_units(near_ref, PLANE - 1, sems.at[1])
        wait_units(near_ref, UNITS - 1, sems.at[0])
        near = jnp.sum(near_ref[...].astype(F32), axis=0).astype(BF)
        far_out_ref[0] = near
        far_ref[me] = near

        @pl.loop(1, SLIDES)
        def _(j):
            pltpu.make_async_remote_copy(
                far_out_ref.at[0], far_ref.at[me], sems.at[2], sems.at[3],
                device_id={"slide": shift(me, j, SLIDES)}, device_id_type=MESH).start()

        wait_units(far_ref, SLIDES - 1, sems.at[3])
        far_out_ref[1] = jnp.sum(far_ref[...].astype(F32), axis=0).astype(BF)
        pltpu.make_async_copy(far_out_ref.at[1], unit_at(res_ref, unit), sems.at[5]).start()

        @pl.loop(1, PLANE)
        def _(j):
            pltpu.make_async_remote_copy(
                far_out_ref.at[1], unit_at(res_ref, unit), sems.at[4], sems.at[5],
                device_id={"tile": shift(tile, j, PLANE)}, device_id_type=MESH).start()

        wait_units(far_ref, SLIDES - 1, sems.at[2])
        wait_units(near_ref, PLANE - 1, sems.at[4])

    @pl.when(jnp.logical_not(owner))
    def _():
        wait_units(near_ref, UNITS, sems.at[0])

    pltpu.make_async_copy(res_ref, res_ref, sems.at[5]).wait()


def sum_kernel(part_ref, kernel_ref, norm_ref, flat_ref, near_ref, far_ref, res_ref, far_out_ref, sems):
    greet(True)
    flat_ref[...] = part_ref[...].astype(BF)
    reduce_all(flat_ref, near_ref, far_ref, res_ref, far_out_ref, sems)
    result = res_ref[...].astype(F32)
    kernel_ref[...] = result[:49]
    norm_ref[...] = result[49:51]


VMEM_LIMIT = 60 * 1024 * 1024


def params(collective_id=None):
    if collective_id is None:
        return pltpu.CompilerParams(vmem_limit_bytes=VMEM_LIMIT)
    return pltpu.CompilerParams(
        vmem_limit_bytes=VMEM_LIMIT, collective_id=collective_id, has_side_effects=True)


def vmem(count):
    return [pl.BlockSpec(memory_space=pltpu.VMEM)] * count


def smem(count):
    return [pl.BlockSpec(memory_space=pltpu.SMEM)] * count


def shape(*dims, kind=BF):
    return jax.ShapeDtypeStruct(dims, kind)


def body(
    tile_maps, dw_kernel, conv_bias, norm_gain, w_in, w_qkv, seg_len, dilation,
    tile_slot, slide_lengths, cotangent,
):
    bias, gain = conv_bias.reshape(1, C), norm_gain.reshape(1, C)
    maps, normed, inverse, total, embed = pl.pallas_call(
        forward_kernel,
        out_shape=[
            shape(SIDE, SIDE, ROWS, C), shape(AREA, ROWS, C), shape(AREA, ROWS, LANE, kind=F32),
            shape(ROWS, C, kind=F32), shape(ROWS, C),
        ],
        in_specs=vmem(5),
        out_specs=vmem(5),
        scratch_shapes=[pltpu.VMEM((49, ROWS, C), BF), pltpu.VMEM((AREA, ROWS, C), F32)],
        compiler_params=params(),
    )(tile_maps, dw_kernel, bias, gain, w_in)
    dma = pltpu.SemaphoreType.DMA
    message = pltpu.VMEM((SLIDES, PACK, LANE), BF)
    attn_out, dpool = pl.pallas_call(
        owner_kernel,
        out_shape=[shape(ROWS, C), shape(ROWS, C, kind=F32)],
        in_specs=vmem(3) + smem(4) + vmem(1),
        out_specs=vmem(2),
        scratch_shapes=[
            pltpu.VMEM((3, HEADS, HEAD, C), BF), message, message, message, message,
            dma((9,)), dma((9,)), dma((9,)), dma((9,)), dma((2, 9)), dma((2, 9)), dma((4,)),
        ],
        compiler_params=params(1),
    )(embed, w_in, w_qkv.T, seg_len, dilation, tile_slot, slide_lengths, cotangent)
    part = pl.pallas_call(
        backward_kernel,
        out_shape=shape(SUM_ROWS, C, kind=F32),
        in_specs=vmem(6),
        out_specs=pl.BlockSpec(memory_space=pltpu.VMEM),
        scratch_shapes=[pltpu.VMEM((AREA, ROWS, C), BF)],
        compiler_params=params(),
    )(dpool, gain, maps, normed, inverse, total)
    grad_kernel, grad_norm = pl.pallas_call(
        sum_kernel,
        out_shape=[shape(49, C, kind=F32), shape(2, C, kind=F32)],
        in_specs=vmem(1),
        out_specs=vmem(2),
        scratch_shapes=[
            pltpu.VMEM((SUM_ROWS, C), BF), pltpu.VMEM((PLANE, 16, LANE), BF),
            pltpu.VMEM((SLIDES, 16, LANE), BF), pltpu.VMEM((SUM_ROWS, C), BF),
            pltpu.VMEM((2, 16, LANE), BF), dma((6,)),
        ],
        compiler_params=params(2),
    )(part)
    return attn_out, grad_kernel, grad_norm


def solution(mesh):
    both = ("tile", "slide")
    in_specs = (
        P(both, None, None, None), P(), P(), P(), P(), P(None, "slide"), P(), P(),
        P(both), P(both, None), P(both, None),
    )
    out_specs = (P(both, None), P(), P())
    return jax.shard_map(body, mesh=mesh, in_specs=in_specs, out_specs=out_specs, check_vma=False)
```

```python
import jax
import jax.numpy as jnp
from jax import lax
from jax.experimental import pallas as pl
from jax.experimental.pallas import tpu as pltpu
from jax.sharding import PartitionSpec as P

NORM_EPS = 1e-06
MESH = pl.DeviceIdType.MESH
BF = jnp.bfloat16
F32 = jnp.float32

SIDE = 8
AREA = SIDE * SIDE
REACH = 3
TAPS = 7
ROWS = 16
C = 768
LANE = 128
CHUNKS = C // LANE
HEADS = 16
HEAD = 48
SLIDES = 16
PLANE = 32
QUOTA = 3
PACK = 32
HALF = C // 2
UNITS = 24
SUM_ROWS = 64


def iota(shape, dim):
    return lax.broadcasted_iota(jnp.int32, shape, dim)


def dot(left, right):
    return jnp.dot(left, right, preferred_element_type=F32)


def dot_last(left, right):
    return lax.dot_general(left, right, (((1,), (1,)), ((), ())), preferred_element_type=F32)


def dot_first(left, right):
    return lax.dot_general(left, right, (((0,), (0,)), ((), ())), preferred_element_type=F32)


def spread(block):
    return jnp.concatenate([block[:, k * LANE : (k + 1) * LANE] for k in range(CHUNKS)], axis=0)


def gather_chunks(stack):
    return jnp.concatenate([stack[k * ROWS : (k + 1) * ROWS] for k in range(CHUNKS)], axis=1)


def row_span(offset):
    return max(0, -offset), min(SIDE, SIDE - offset)


def map_copy(maps_ref, rows_ref, sems, r):
    return pltpu.make_async_copy(maps_ref.at[:, r], rows_ref.at[r], sems.at[r])


def transpose_maps(maps_ref, rows_ref, sems, xt_ref):
    row, col = iota((128, 128), 0), iota((128, 128), 1)
    perm = ((row >> 4) == (col & 7)) & ((row & 15) == (col >> 3))
    perm = perm.astype(F32).astype(BF)
    for r in range(SIDE):
        map_copy(maps_ref, rows_ref, sems, r).wait()
        part = rows_ref[r].astype(F32).reshape(128, C).astype(BF)
        xt_ref[r] = dot(perm, part).reshape(SIDE, ROWS, C)


def spread_taps(dw_ref, wb_ref):
    taps = dw_ref[...].astype(F32)
    for tap in range(TAPS * TAPS):
        wb_ref[tap] = jnp.broadcast_to(taps[tap : tap + 1], (8, C))


def conv_chunk(chunk, xt_ref, wb_ref, bias_ref, cv_ref):
    lanes = pl.ds(pl.multiple_of(chunk * LANE, LANE), LANE)
    bias = jnp.broadcast_to(bias_ref[lanes].reshape(1, LANE), (2, 8, LANE))
    for i in range(SIDE):
        total = [bias] * SIDE
        for r in range(TAPS):
            src = i + r - REACH
            if not 0 <= src < SIDE:
                continue
            cells = [xt_ref[src, j, :, lanes].reshape(2, 8, LANE) for j in range(SIDE)]
            taps = [wb_ref[r * TAPS + s, :, lanes] for s in range(TAPS)]
            for j in range(SIDE):
                for s in range(TAPS):
                    at = j + s - REACH
                    if 0 <= at < SIDE:
                        total[j] = total[j] + cells[at] * taps[s]
        for j in range(SIDE):
            cv_ref[i * SIDE + j, :, lanes] = total[j].reshape(ROWS, LANE)


def normalise(cv_ref, inv_ref, rows, total):
    def step(b, total):
        some = pl.ds(b * SIDE, SIDE)
        mean = jnp.mean(cv_ref[some], axis=2, keepdims=True)
        centered = cv_ref[some] - mean
        inv = lax.rsqrt(jnp.mean(centered * centered, axis=2, keepdims=True) + NORM_EPS)
        normed = (cv_ref[some] - mean) * inv
        cv_ref[some] = normed
        inv_ref[some] = jnp.broadcast_to(inv, (SIDE, ROWS, LANE))
        return total + jnp.sum(normed, axis=0)

    return lax.fori_loop(rows[0], rows[1], step, total)


def send_rows(slot_ref):
    lane = iota((1, 112), 1)
    tile, chunk = lane & 15, lane >> 4
    owner = jnp.zeros((1, 112), jnp.int32)
    for t in range(ROWS):
        owner = jnp.where(tile == t, slot_ref[t] >> 4, owner)
    rank = jnp.zeros((1, 112), jnp.int32)
    for t in range(ROWS):
        rank = rank + jnp.where((owner == (slot_ref[t] >> 4)) & (tile > t), 1, 0)
    want = owner * PACK + chunk * QUOTA + rank
    select = (iota((SLIDES * PACK, 112), 0) == want).astype(F32).astype(BF)
    sub = iota((ROWS, LANE), 0)
    slots = jnp.zeros((ROWS, LANE), jnp.int32)
    for t in range(ROWS):
        slots = jnp.where(sub == t, (slot_ref[t] & 15) + 1, slots)
    return select, slots.astype(F32).astype(BF)


def slot_spread():
    size = SLIDES * PACK
    row, col = iota((size, size), 0), iota((size, size), 1)
    inside = row & (PACK - 1)
    quota = inside
    for k in range(1, PACK // QUOTA + 1):
        quota = jnp.where(inside >= k * QUOTA, inside - k * QUOTA, quota)
    return (col == (row - inside + CHUNKS * QUOTA + quota)).astype(F32).astype(BF)


def place_rows(spread_slots, arrived):
    size = SLIDES * PACK
    slot = dot(spread_slots, arrived)[:, : CHUNKS * ROWS]
    inside = iota((size, CHUNKS * ROWS), 0) & (PACK - 1)
    lane = iota((size, CHUNKS * ROWS), 1)
    first = (lane >> 4) * QUOTA
    want = ((lane & 15) + 1).astype(F32)
    hit = (inside >= first) & (inside < first + QUOTA) & (slot == want)
    return hit.astype(F32).astype(BF)


def head_mask():
    row, lane = iota((HEADS * ROWS, C), 0), iota((HEADS * ROWS, C), 1)
    low = (row >> 4) * HEAD
    return ((lane >= low) & (lane < low + HEAD)).astype(F32).astype(BF)


def allowed_pairs(seg_ref, dil_ref, len_ref):
    left, right = iota((ROWS, ROWS), 0), iota((ROWS, ROWS), 1)
    cut = len_ref[0, 0]
    run_left, run_right = left >= cut, right >= cut
    pos_left = jnp.where(run_left, left - cut, left)
    pos_right = jnp.where(run_right, right - cut, right)
    apart = pos_left ^ pos_right
    apart = jnp.where(run_left != run_right, apart | 256, apart)
    parts = []
    for h in range(HEADS):
        parts.append(apart & (~(seg_ref[h] - 1) | (dil_ref[h] - 1)))
    return jnp.concatenate(parts, axis=0) == 0


def attention(block, w3_ref, cot_ref, attn_ref, mask, allowed):
    scale = HEAD ** (-0.5)
    weights = [w3_ref[part].reshape(C, C) for part in range(3)]
    query, key, value = [dot_last(block, each).astype(BF) for each in weights]
    many_query = jnp.concatenate([query] * HEADS, axis=0) * mask
    many_grad = jnp.concatenate([cot_ref[...]] * HEADS, axis=0) * mask
    scores = dot_last(many_query, key) * scale
    masked = jnp.where(allowed, scores, -1e30)
    top = jnp.max(masked, axis=1, keepdims=True)
    expo = jnp.where(allowed, jnp.exp(masked - top), 0.0)
    prob = expo / jnp.sum(expo, axis=1, keepdims=True)
    prob_bf = prob.astype(BF)
    mask_f = mask.astype(F32)

    def own_head(full):
        return jnp.sum((full * mask_f).reshape(HEADS, ROWS, C), axis=0)

    attn_ref[...] = own_head(dot(prob_bf, value)).astype(BF)
    dprob = dot_last(many_grad, value)
    dscore = (prob * (dprob - jnp.sum(prob * dprob, axis=1, keepdims=True)) * scale).astype(BF)
    dquery = own_head(dot(dscore, key)).astype(BF)
    dkey = dot_first(dscore, many_query).astype(BF)
    dvalue = dot_first(prob_bf, many_grad).astype(BF)
    total = dot(dquery, weights[0]) + dot(dkey, weights[1]) + dot(dvalue, weights[2])
    return total.astype(BF)


def shift(index, by, size):
    return (index + by + size) & (size - 1)


def core_of(tile):
    return tile & 1


class Ring:
    def __init__(self, w3_ref, sems):
        self.w3_ref = w3_ref
        self.right, self.left, self.core = sems[0:2], sems[2:4], sems[4:6]
        tile = lax.axis_index("tile")
        self.me = lax.axis_index("slide")
        self.lanes = pl.ds(pl.multiple_of(core_of(tile) * HALF, HALF), HALF)
        self.other = tile + 1 - 2 * core_of(tile)

    def copy(self, head, send_sem, recv_sem, device):
        block = self.w3_ref.at[:, head, :, self.lanes]
        return pltpu.make_async_remote_copy(
            block, block, send_sem, recv_sem, device_id=device, device_id_type=MESH)

    def to_right(self, s):
        return self.copy(
            shift(self.me, -s, SLIDES), self.right[0].at[s], self.right[1].at[s],
            {"slide": shift(self.me, 1, SLIDES)})

    def to_left(self, s):
        return self.copy(
            shift(self.me, s, SLIDES), self.left[0].at[s], self.left[1].at[s],
            {"slide": shift(self.me, -1, SLIDES)})

    def left_to_core(self, s):
        return self.copy(
            shift(self.me, -s, SLIDES), self.core[0].at[0, s], self.core[1].at[0, s],
            {"tile": self.other})

    def right_to_core(self, s):
        return self.copy(
            shift(self.me, s, SLIDES), self.core[0].at[1, s], self.core[1].at[1, s],
            {"tile": self.other})


RIGHT_STEPS = SLIDES // 2
LEFT_STEPS = SLIDES // 2 - 1


def ring_start(wq_ref, w3_ref, ring):
    w3_ref[:, ring.me] = wq_ref[...].reshape(3, HEAD, C)
    ring.to_right(0).start()
    ring.to_left(0).start()


def ring_step(ring, s, inner=False):
    ring.to_right(s - 1).wait_recv()
    if inner or s < RIGHT_STEPS:
        ring.to_right(s).start()
    ring.left_to_core(s).start()
    if inner or s <= LEFT_STEPS:
        ring.to_left(s - 1).wait_recv()
        if inner or s < LEFT_STEPS:
            ring.to_left(s).start()
        ring.right_to_core(s).start()


def ring_end(ring):
    for s in range(RIGHT_STEPS + 1):
        if s >= 1:
            ring.left_to_core(s).wait()
        if 1 <= s <= LEFT_STEPS:
            ring.right_to_core(s).wait()
        if s < RIGHT_STEPS:
            ring.to_right(s).wait_send()
        if s < LEFT_STEPS:
            ring.to_left(s).wait_send()


def exchange_start(out_ref, in_ref, send_sem, recv_sem):
    me = lax.axis_index("slide")
    in_ref[me] = out_ref[me]

    @pl.loop(1, SLIDES)
    def _(j):
        peer = shift(me, j, SLIDES)
        pltpu.make_async_remote_copy(
            out_ref.at[peer], in_ref.at[me], send_sem, recv_sem,
            device_id={"slide": peer}, device_id_type=MESH).start()


def exchange_wait(out_ref, in_ref, send_sem, recv_sem):
    some = pl.ds(0, SLIDES - 1)
    pltpu.make_async_copy(in_ref.at[some], in_ref.at[some], recv_sem).wait()
    pltpu.make_async_copy(out_ref.at[some], out_ref.at[some], send_sem).wait()


def greet():
    tile, me = lax.axis_index("tile"), lax.axis_index("slide")
    barrier = pltpu.get_barrier_semaphore()

    @pl.loop(1, SLIDES)
    def _(j):
        pl.semaphore_signal(
            barrier, inc=1, device_id={"slide": shift(me, j, SLIDES)}, device_id_type=MESH)

    @pl.loop(1, PLANE)
    def _(j):
        pl.semaphore_signal(
            barrier, inc=1, device_id={"tile": shift(tile, j, PLANE)}, device_id_type=MESH)


def greeted():
    pl.semaphore_wait(pltpu.get_barrier_semaphore(), SLIDES + PLANE - 2)


def conv_grads(dpool, gain, cv_ref, inv_ref):
    grad = dpool * (gain * (1.0 / AREA))
    level = grad - jnp.mean(grad, axis=1, keepdims=True)

    def step(b, total):
        some = pl.ds(b * SIDE, SIDE)
        along = jnp.mean(cv_ref[some] * grad, axis=2, keepdims=True)
        dconv = inv_ref[some][:, :, :1] * (level - cv_ref[some] * along)
        cv_ref[some] = dconv
        return total + jnp.sum(dconv, axis=0)

    return lax.fori_loop(0, SIDE, step, jnp.zeros((ROWS, C), F32))


def tap_grads(chunk, xt_ref, cv_ref, part_ref):
    lanes = pl.ds(pl.multiple_of(chunk * LANE, LANE), LANE)
    for r in range(TAPS):
        total = [jnp.zeros((ROWS, LANE), F32)] * TAPS
        for i in range(*row_span(r - REACH)):
            cells = [xt_ref[i + r - REACH, j, :, lanes] for j in range(SIDE)]
            grads = [cv_ref[i * SIDE + j, :, lanes] for j in range(SIDE)]
            for s in range(TAPS):
                for j in range(*row_span(s - REACH)):
                    total[s] = total[s] + cells[j + s - REACH] * grads[j]
        for s in range(TAPS):
            tap = r * TAPS + s
            part_ref[tap : tap + 1, lanes] = jnp.sum(total[s], axis=0, keepdims=True)


def unit_at(ref, unit):
    rows = pl.ds(pl.multiple_of((unit & 3) * 16, 16), 16)
    lanes = pl.ds(pl.multiple_of((unit >> 2) * LANE, LANE), LANE)
    return ref.at[rows, lanes]


def owner_of(unit):
    return unit + ((unit * 11) >> 5)


def reduce_all(flat_ref, near_ref, far_ref, res_ref, far_out_ref, sems):
    tile, me = lax.axis_index("tile"), lax.axis_index("slide")
    owner = (tile & 3) != 3
    unit = jnp.minimum((tile >> 2) * 3 + (tile & 3), UNITS - 1)

    @pl.loop(0, UNITS)
    def _(j):
        peer = owner_of(j)

        @pl.when(peer != tile)
        def _():
            pltpu.make_async_remote_copy(
                unit_at(flat_ref, j), near_ref.at[tile], sems.at[0], sems.at[1],
                device_id={"tile": peer}, device_id_type=MESH).start()

    def wait_units(ref, count, sem):
        some = pl.ds(0, count)
        pltpu.make_async_copy(ref.at[some], ref.at[some], sem).wait()

    @pl.when(owner)
    def _():
        near_ref[tile] = unit_at(flat_ref, unit)[...]
        wait_units(near_ref, PLANE - 1, sems.at[1])
        wait_units(near_ref, UNITS - 1, sems.at[0])
        near = jnp.sum(near_ref[...].astype(F32), axis=0).astype(BF)
        far_out_ref[0] = near
        far_ref[me] = near

        @pl.loop(1, SLIDES)
        def _(j):
            pltpu.make_async_remote_copy(
                far_out_ref.at[0], far_ref.at[me], sems.at[2], sems.at[3],
                device_id={"slide": shift(me, j, SLIDES)}, device_id_type=MESH).start()

        wait_units(far_ref, SLIDES - 1, sems.at[3])
        far_out_ref[1] = jnp.sum(far_ref[...].astype(F32), axis=0).astype(BF)
        pltpu.make_async_copy(far_out_ref.at[1], unit_at(res_ref, unit), sems.at[5]).start()

        @pl.loop(1, PLANE)
        def _(j):
            pltpu.make_async_remote_copy(
                far_out_ref.at[1], unit_at(res_ref, unit), sems.at[4], sems.at[5],
                device_id={"tile": shift(tile, j, PLANE)}, device_id_type=MESH).start()

        wait_units(far_ref, SLIDES - 1, sems.at[2])
        wait_units(near_ref, PLANE - 1, sems.at[4])

    @pl.when(jnp.logical_not(owner))
    def _():
        wait_units(near_ref, UNITS, sems.at[0])

    pltpu.make_async_copy(res_ref, res_ref, sems.at[5]).wait()


def step_kernel(
    maps_ref, dw_ref, bias_ref, gain_ref, win_hbm, wq_ref, seg_ref, dil_ref, slot_ref, len_ref, cot_ref,
    attn_ref, sums_ref,
    rows_ref, xt_ref, cv_ref, inv_ref, wb_ref, win_ref, w3_ref,
    out_ref, in_ref, back_out_ref, back_in_ref,
    part_ref, flat_ref, near_ref, far_ref, far_out_ref, res_ref,
    local_sems, right_send, right_recv, left_send, left_recv, core_send, core_recv, route_sems, sum_sems,
):
    greet()
    for r in range(SIDE):
        map_copy(maps_ref, rows_ref, local_sems, r).start()
    win_copy = pltpu.make_async_copy(win_hbm, win_ref, local_sems.at[SIDE])
    win_copy.start()
    ring = Ring(w3_ref, (right_send, right_recv, left_send, left_recv, core_send, core_recv))
    w3_ref[:, ring.me] = wq_ref[...].reshape(3, HEAD, C)
    spread_taps(dw_ref, wb_ref)
    greeted()
    ring.to_right(0).start()
    ring.to_left(0).start()
    transpose_maps(maps_ref, rows_ref, local_sems, xt_ref)

    @pl.loop(0, 2)
    def _(half):
        @pl.loop(0, CHUNKS // 2)
        def _(chunk):
            conv_chunk(half * (CHUNKS // 2) + chunk, xt_ref, wb_ref, bias_ref, cv_ref)

        ring_step(ring, half + 1, True)

    total = normalise(cv_ref, inv_ref, (0, SIDE), jnp.zeros((ROWS, C), F32))
    ring_step(ring, 3)
    gain = gain_ref[...].reshape(1, C)
    pooled = (total * gain * (1.0 / AREA)).astype(BF)
    win_copy.wait()
    embed = dot(pooled, win_ref[...]).astype(BF)

    select, slots = send_rows(slot_ref)
    packed = jnp.concatenate([spread(embed), slots], axis=0)
    out_ref[...] = dot(select, packed).astype(BF).reshape(SLIDES, PACK, LANE)
    exchange_start(out_ref, in_ref, route_sems.at[0], route_sems.at[1])
    spread_slots, mask = slot_spread(), head_mask()
    allowed = allowed_pairs(seg_ref, dil_ref, len_ref)
    for s in range(4, RIGHT_STEPS + 1):
        ring_step(ring, s)
    exchange_wait(out_ref, in_ref, route_sems.at[0], route_sems.at[1])
    arrived = in_ref[...].reshape(SLIDES * PACK, LANE)
    place = place_rows(spread_slots, arrived)
    block = gather_chunks(dot_first(place, arrived).astype(BF))
    ring_end(ring)
    dblock = attention(block, w3_ref, cot_ref, attn_ref, mask, allowed)
    back_out_ref[...] = dot(place, spread(dblock)).astype(BF).reshape(SLIDES, PACK, LANE)
    exchange_start(back_out_ref, back_in_ref, route_sems.at[2], route_sems.at[3])
    exchange_wait(back_out_ref, back_in_ref, route_sems.at[2], route_sems.at[3])
    returned = back_in_ref[...].reshape(SLIDES * PACK, LANE)
    dembed = gather_chunks(dot_first(select[:, : CHUNKS * ROWS], returned).astype(BF))
    dpool = dot_last(dembed, win_ref[...])

    bias_grad = conv_grads(dpool, gain, cv_ref, inv_ref)
    part_ref[...] = jnp.zeros(part_ref.shape, F32)
    part_ref[49:50] = jnp.sum(bias_grad, axis=0, keepdims=True)
    part_ref[50:51] = jnp.sum(dpool * total, axis=0, keepdims=True) * (1.0 / AREA)

    @pl.loop(0, CHUNKS)
    def _(chunk):
        tap_grads(chunk, xt_ref, cv_ref, part_ref)

    flat_ref[...] = part_ref[...].astype(BF)
    reduce_all(flat_ref, near_ref, far_ref, res_ref, far_out_ref, sum_sems)
    sums_ref[...] = res_ref[...]


def finish_kernel(attn_ref, res_ref, out_ref, kernel_ref, norm_ref):
    out_ref[...] = attn_ref[...]
    result = res_ref[...].astype(F32)
    kernel_ref[...] = result[:49]
    norm_ref[...] = result[49:51]


VMEM_LIMIT = 60 * 1024 * 1024


def params(**extra):
    return pltpu.CompilerParams(vmem_limit_bytes=VMEM_LIMIT, **extra)


def vmem(count):
    return [pl.BlockSpec(memory_space=pltpu.VMEM)] * count


def smem(count):
    return [pl.BlockSpec(memory_space=pltpu.SMEM)] * count


def shape(*dims, kind=BF):
    return jax.ShapeDtypeStruct(dims, kind)


def body(
    tile_maps, dw_kernel, conv_bias, norm_gain, w_in, w_qkv, seg_len, dilation,
    tile_slot, slide_lengths, cotangent,
):
    dma = pltpu.SemaphoreType.DMA
    hbm = [pl.BlockSpec(memory_space=pl.ANY)]
    message = pltpu.VMEM((SLIDES, PACK, LANE), BF)
    attn, sums = pl.pallas_call(
        step_kernel,
        out_shape=[shape(ROWS, C), shape(SUM_ROWS, C)],
        in_specs=hbm + vmem(3) + hbm + vmem(1) + smem(4) + vmem(1),
        out_specs=vmem(2),
        scratch_shapes=[
            pltpu.VMEM((SIDE, ROWS, SIDE, C), BF), pltpu.VMEM((SIDE, SIDE, ROWS, C), F32),
            pltpu.VMEM((AREA, ROWS, C), F32), pltpu.VMEM((AREA, ROWS, LANE), F32),
            pltpu.VMEM((49, 8, C), F32), pltpu.VMEM((C, C), BF),
            pltpu.VMEM((3, HEADS, HEAD, C), BF), message, message, message, message,
            pltpu.VMEM((SUM_ROWS, C), F32), pltpu.VMEM((SUM_ROWS, C), BF),
            pltpu.VMEM((PLANE, 16, LANE), BF), pltpu.VMEM((SLIDES, 16, LANE), BF),
            pltpu.VMEM((2, 16, LANE), BF), pltpu.VMEM((SUM_ROWS, C), BF),
            dma((9,)), dma((9,)), dma((9,)), dma((9,)), dma((9,)), dma((2, 9)), dma((2, 9)), dma((4,)),
            dma((6,)),
        ],
        compiler_params=params(collective_id=1, has_side_effects=True),
    )(
        tile_maps, dw_kernel, conv_bias, norm_gain, w_in, w_qkv.T,
        seg_len, dilation, tile_slot, slide_lengths, cotangent,
    )
    return pl.pallas_call(
        finish_kernel,
        out_shape=[shape(ROWS, C), shape(49, C, kind=F32), shape(2, C, kind=F32)],
        in_specs=vmem(2),
        out_specs=vmem(3),
    )(attn, sums)


def solution(mesh):
    both = ("tile", "slide")
    in_specs = (
        P(both, None, None, None), P(), P(), P(), P(), P(None, "slide"), P(), P(),
        P(both), P(both, None), P(both, None),
    )
    out_specs = (P(both, None), P(), P())
    return jax.shard_map(body, mesh=mesh, in_specs=in_specs, out_specs=out_specs, check_vma=False)
```

```python
import jax
import jax.numpy as jnp
from jax import lax
from jax.experimental import pallas as pl
from jax.experimental.pallas import tpu as pltpu
from jax.sharding import PartitionSpec as P

NORM_EPS = 1e-06
MESH = pl.DeviceIdType.MESH
BF = jnp.bfloat16
F32 = jnp.float32

SIDE = 8
AREA = SIDE * SIDE
REACH = 3
TAPS = 7
ROWS = 16
C = 768
LANE = 128
CHUNKS = C // LANE
HEADS = 16
HEAD = 48
SLIDES = 16
PLANE = 32
QUOTA = 3
PACK = 32
MEMBERS = 8
SHARE = HEADS // MEMBERS
WIDE = MEMBERS * ROWS
COLS = SHARE * HEAD
UNITS = 24
SUM_ROWS = 64


def iota(shape, dim):
    return lax.broadcasted_iota(jnp.int32, shape, dim)


def dot(left, right):
    return jnp.dot(left, right, preferred_element_type=F32)


def dot_last(left, right):
    return lax.dot_general(left, right, (((1,), (1,)), ((), ())), preferred_element_type=F32)


def dot_first(left, right):
    return lax.dot_general(left, right, (((0,), (0,)), ((), ())), preferred_element_type=F32)


def spread(block):
    return jnp.concatenate([block[:, k * LANE : (k + 1) * LANE] for k in range(CHUNKS)], axis=0)


def gather_chunks(stack):
    return jnp.concatenate([stack[k * ROWS : (k + 1) * ROWS] for k in range(CHUNKS)], axis=1)


def row_span(offset):
    return max(0, -offset), min(SIDE, SIDE - offset)


def map_copy(maps_ref, rows_ref, sems, r):
    return pltpu.make_async_copy(maps_ref.at[:, r], rows_ref.at[r], sems.at[r])


def transpose_maps(maps_ref, rows_ref, sems, xt_ref):
    row, col = iota((128, 128), 0), iota((128, 128), 1)
    perm = ((row >> 4) == (col & 7)) & ((row & 15) == (col >> 3))
    perm = perm.astype(F32).astype(BF)
    for r in range(SIDE):
        map_copy(maps_ref, rows_ref, sems, r).wait()
        part = rows_ref[r].astype(F32).reshape(128, C).astype(BF)
        xt_ref[r] = dot(perm, part).reshape(SIDE, ROWS, C)


def spread_taps(dw_ref, wb_ref):
    taps = dw_ref[...].astype(F32)
    for tap in range(TAPS * TAPS):
        wb_ref[tap] = jnp.broadcast_to(taps[tap : tap + 1], (8, C))


def conv_chunk(chunk, xt_ref, wb_ref, bias_ref, cv_ref):
    lanes = pl.ds(pl.multiple_of(chunk * LANE, LANE), LANE)
    bias = jnp.broadcast_to(bias_ref[lanes].reshape(1, LANE), (2, 8, LANE))
    for i in range(SIDE):
        total = [bias] * SIDE
        for r in range(TAPS):
            src = i + r - REACH
            if not 0 <= src < SIDE:
                continue
            cells = [xt_ref[src, j, :, lanes].reshape(2, 8, LANE) for j in range(SIDE)]
            taps = [wb_ref[r * TAPS + s, :, lanes] for s in range(TAPS)]
            for j in range(SIDE):
                for s in range(TAPS):
                    at = j + s - REACH
                    if 0 <= at < SIDE:
                        total[j] = total[j] + cells[at] * taps[s]
        for j in range(SIDE):
            cv_ref[i * SIDE + j, :, lanes] = total[j].reshape(ROWS, LANE)


def normalise(cv_ref, inv_ref, rows, total):
    def step(b, total):
        some = pl.ds(b * SIDE, SIDE)
        mean = jnp.mean(cv_ref[some], axis=2, keepdims=True)
        centered = cv_ref[some] - mean
        inv = lax.rsqrt(jnp.mean(centered * centered, axis=2, keepdims=True) + NORM_EPS)
        normed = (cv_ref[some] - mean) * inv
        cv_ref[some] = normed
        inv_ref[some] = jnp.broadcast_to(inv, (SIDE, ROWS, LANE))
        return total + jnp.sum(normed, axis=0)

    return lax.fori_loop(rows[0], rows[1], step, total)


def send_rows(slot_ref):
    lane = iota((1, 112), 1)
    tile, chunk = lane & 15, lane >> 4
    owner = jnp.zeros((1, 112), jnp.int32)
    for t in range(ROWS):
        owner = jnp.where(tile == t, slot_ref[t] >> 4, owner)
    rank = jnp.zeros((1, 112), jnp.int32)
    for t in range(ROWS):
        rank = rank + jnp.where((owner == (slot_ref[t] >> 4)) & (tile > t), 1, 0)
    want = owner * PACK + chunk * QUOTA + rank
    select = (iota((SLIDES * PACK, 112), 0) == want).astype(F32).astype(BF)
    sub = iota((ROWS, LANE), 0)
    slots = jnp.zeros((ROWS, LANE), jnp.int32)
    for t in range(ROWS):
        slots = jnp.where(sub == t, (slot_ref[t] & 15) + 1, slots)
    return select, slots.astype(F32).astype(BF)


def slot_spread():
    size = SLIDES * PACK
    row, col = iota((size, size), 0), iota((size, size), 1)
    inside = row & (PACK - 1)
    quota = inside
    for k in range(1, PACK // QUOTA + 1):
        quota = jnp.where(inside >= k * QUOTA, inside - k * QUOTA, quota)
    return (col == (row - inside + CHUNKS * QUOTA + quota)).astype(F32).astype(BF)


def place_rows(spread_slots, arrived):
    size = SLIDES * PACK
    slot = dot(spread_slots, arrived)[:, : CHUNKS * ROWS]
    inside = iota((size, CHUNKS * ROWS), 0) & (PACK - 1)
    lane = iota((size, CHUNKS * ROWS), 1)
    first = (lane >> 4) * QUOTA
    want = ((lane & 15) + 1).astype(F32)
    hit = (inside >= first) & (inside < first + QUOTA) & (slot == want)
    return hit.astype(F32).astype(BF)


def head_mask():
    row, lane = iota((SHARE * WIDE, COLS), 0), iota((SHARE * WIDE, COLS), 1)
    low = jnp.where(row >= WIDE, HEAD, 0)
    return ((lane >= low) & (lane < low + HEAD)).astype(F32).astype(BF)


def member_columns():
    row, col = iota((C, MEMBERS * LANE), 0), iota((C, MEMBERS * LANE), 1)
    lane = col & (LANE - 1)
    first = (col >> 7) * HEAD + lane
    want = jnp.where(lane < HEAD, first, first + (MEMBERS - 1) * HEAD)
    want = jnp.where(lane < COLS, want, -1)
    return (row == want).astype(F32).astype(BF)


def allowed_pairs(member, seg_ref, dil_ref, cut):
    left, right = iota((WIDE, WIDE), 0), iota((WIDE, WIDE), 1)
    slot_left, slot_right = left & 15, right & 15
    run_left, run_right = slot_left >= cut, slot_right >= cut
    pos_left = jnp.where(run_left, slot_left - cut, slot_left)
    pos_right = jnp.where(run_right, slot_right - cut, slot_right)
    apart = pos_left ^ pos_right
    apart = jnp.where(run_left != run_right, apart | 256, apart)
    apart = jnp.where((left >> 4) != (right >> 4), apart | 256, apart)
    parts = []
    for h in range(SHARE):
        seg, dil = seg_ref[member + MEMBERS * h], dil_ref[member + MEMBERS * h]
        parts.append(apart & (~(seg - 1) | (dil - 1)))
    return jnp.concatenate(parts, axis=0) == 0


def attention(block, upstream, w3_ref, mask, allowed):
    scale = HEAD ** (-0.5)
    weights = [w3_ref[part].reshape(COLS, C) for part in range(3)]
    query, key, value = [dot_last(block, each).astype(BF) for each in weights]
    many_query = jnp.concatenate([query] * SHARE, axis=0) * mask
    many_grad = jnp.concatenate([upstream] * SHARE, axis=0) * mask
    scores = dot_last(many_query, key) * scale
    masked = jnp.where(allowed, scores, -1e30)
    top = jnp.max(masked, axis=1, keepdims=True)
    expo = jnp.where(allowed, jnp.exp(masked - top), 0.0)
    prob = expo / jnp.sum(expo, axis=1, keepdims=True)
    prob_bf = prob.astype(BF)
    mask_f = mask.astype(F32)

    def own_head(full):
        return jnp.sum((full * mask_f).reshape(SHARE, WIDE, COLS), axis=0)

    mixed = own_head(dot(prob_bf, value))
    dprob = dot_last(many_grad, value)
    dscore = (prob * (dprob - jnp.sum(prob * dprob, axis=1, keepdims=True)) * scale).astype(BF)
    dquery = own_head(dot(dscore, key)).astype(BF)
    dkey = dot_first(dscore, many_query).astype(BF)
    dvalue = dot_first(prob_bf, many_grad).astype(BF)
    total = dot(dquery, weights[0]) + dot(dkey, weights[1]) + dot(dvalue, weights[2])
    return mixed, total


def shift(index, by, size):
    return (index + by + size) & (size - 1)


class Weights:
    def __init__(self, w3_ref, send_sems, recv_sems, share_sems):
        self.w3_ref, self.send, self.recv, self.share = w3_ref, send_sems, recv_sems, share_sems
        self.tile, self.me = lax.axis_index("tile"), lax.axis_index("slide")
        self.y = (self.tile >> 1) & 3
        self.member = (self.tile >> 3) * 2 + (self.tile & 1)
        self.carrier = self.y < 3
        self.row = pl.multiple_of(jnp.minimum(self.y, 2) * 16, 16)
        self.source = self.carrier & ((self.me & 7) == self.member)

    def along_z(self, j):
        head = self.me >> 3
        rows = self.w3_ref.at[:, head, pl.ds(self.row, 16)]
        return pltpu.make_async_remote_copy(
            rows, rows, self.send.at[j], self.recv.at[head],
            device_id={"slide": shift(self.me, j, SLIDES)}, device_id_type=MESH)

    def along_y(self, j):
        peer = (self.tile & ~6) | (((self.y + j) & 3) << 1)
        rows = self.w3_ref.at[:, :, pl.ds(self.row, 16)]
        return pltpu.make_async_remote_copy(
            rows, rows, self.share.at[3 + j], self.share.at[jnp.minimum(self.y, 2)],
            device_id={"tile": peer}, device_id_type=MESH)

    def start(self, wq_ref):
        @pl.when(self.source)
        def _():
            for part in range(3):
                self.w3_ref[part, self.me >> 3, pl.ds(self.row, 16)] = wq_ref[
                    pl.ds(pl.multiple_of(part * HEAD + self.row, 16), 16)]

            @pl.loop(1, SLIDES)
            def _(j):
                self.along_z(j).start()

    def hand_on(self):
        @pl.when(self.carrier)
        def _():
            for head in range(SHARE):

                @pl.when(self.me != self.member + MEMBERS * head)
                def _():
                    rows = self.w3_ref.at[:, head, pl.ds(0, 16)]
                    pltpu.make_async_copy(rows, rows, self.recv.at[head]).wait()

            for j in range(1, 4):
                self.along_y(j).start()

    def finish(self):
        for y in range(3):

            @pl.when(self.y != y)
            def _():
                rows = self.w3_ref.at[:, :, pl.ds(16 * y, 16)]
                pltpu.make_async_copy(rows, rows, self.share.at[y]).wait()

    def end(self):
        @pl.when(self.source)
        def _():
            @pl.loop(1, SLIDES)
            def _(j):
                self.along_z(j).wait_send()

        @pl.when(self.carrier)
        def _():
            for j in range(1, 4):
                self.along_y(j).wait_send()


def members_start(out_ref, in_ref, sems, n, same=False):
    tile = lax.axis_index("tile")
    member = (tile >> 3) * 2 + (tile & 1)
    if not same:
        in_ref[member] = out_ref[member]

    @pl.loop(1, MEMBERS)
    def _(j):
        peer = shift(member, j, MEMBERS)
        pltpu.make_async_remote_copy(
            in_ref.at[member] if same else out_ref.at[peer], in_ref.at[member],
            sems.at[0, n], sems.at[1, n],
            device_id={"tile": (peer >> 1) * 8 + (tile & 6) + (peer & 1)}, device_id_type=MESH).start()


def members_wait(in_ref, sems, n):
    some = in_ref.at[pl.ds(0, MEMBERS - 1)]
    pltpu.make_async_copy(some, some, sems.at[1, n]).wait()
    pltpu.make_async_copy(some, some, sems.at[0, n]).wait()


def exchange_start(out_ref, in_ref, send_sem, recv_sem):
    me = lax.axis_index("slide")
    in_ref[me] = out_ref[me]

    @pl.loop(1, SLIDES)
    def _(j):
        peer = shift(me, j, SLIDES)
        pltpu.make_async_remote_copy(
            out_ref.at[peer], in_ref.at[me], send_sem, recv_sem,
            device_id={"slide": peer}, device_id_type=MESH).start()


def exchange_wait(out_ref, in_ref, send_sem, recv_sem):
    some = pl.ds(0, SLIDES - 1)
    pltpu.make_async_copy(in_ref.at[some], in_ref.at[some], recv_sem).wait()
    pltpu.make_async_copy(out_ref.at[some], out_ref.at[some], send_sem).wait()


def greet():
    tile, me = lax.axis_index("tile"), lax.axis_index("slide")
    barrier = pltpu.get_barrier_semaphore()

    @pl.loop(1, SLIDES)
    def _(j):
        pl.semaphore_signal(
            barrier, inc=1, device_id={"slide": shift(me, j, SLIDES)}, device_id_type=MESH)

    @pl.loop(1, PLANE)
    def _(j):
        pl.semaphore_signal(
            barrier, inc=1, device_id={"tile": shift(tile, j, PLANE)}, device_id_type=MESH)


def greeted():
    pl.semaphore_wait(pltpu.get_barrier_semaphore(), SLIDES + PLANE - 2)


def conv_grads(dpool, gain, cv_ref, inv_ref):
    grad = dpool * (gain * (1.0 / AREA))
    level = grad - jnp.mean(grad, axis=1, keepdims=True)

    def step(b, total):
        some = pl.ds(b * SIDE, SIDE)
        along = jnp.mean(cv_ref[some] * grad, axis=2, keepdims=True)
        dconv = inv_ref[some][:, :, :1] * (level - cv_ref[some] * along)
        cv_ref[some] = dconv
        return total + jnp.sum(dconv, axis=0)

    return lax.fori_loop(0, SIDE, step, jnp.zeros((ROWS, C), F32))


def tap_grads(chunk, xt_ref, cv_ref, part_ref):
    lanes = pl.ds(pl.multiple_of(chunk * LANE, LANE), LANE)
    for r in range(TAPS):
        total = [jnp.zeros((ROWS, LANE), F32)] * TAPS
        for i in range(*row_span(r - REACH)):
            cells = [xt_ref[i + r - REACH, j, :, lanes] for j in range(SIDE)]
            grads = [cv_ref[i * SIDE + j, :, lanes] for j in range(SIDE)]
            for s in range(TAPS):
                for j in range(*row_span(s - REACH)):
                    total[s] = total[s] + cells[j + s - REACH] * grads[j]
        for s in range(TAPS):
            tap = r * TAPS + s
            part_ref[tap : tap + 1, lanes] = jnp.sum(total[s], axis=0, keepdims=True)


def unit_at(ref, unit):
    rows = pl.ds(pl.multiple_of((unit & 3) * 16, 16), 16)
    lanes = pl.ds(pl.multiple_of((unit >> 2) * LANE, LANE), LANE)
    return ref.at[rows, lanes]


def owner_of(unit):
    return unit + ((unit * 11) >> 5)


def reduce_all(flat_ref, near_ref, far_ref, res_ref, far_out_ref, sems):
    tile, me = lax.axis_index("tile"), lax.axis_index("slide")
    owner = (tile & 3) != 3
    unit = jnp.minimum((tile >> 2) * 3 + (tile & 3), UNITS - 1)

    @pl.loop(0, UNITS)
    def _(j):
        peer = owner_of(j)

        @pl.when(peer != tile)
        def _():
            pltpu.make_async_remote_copy(
                unit_at(flat_ref, j), near_ref.at[tile], sems.at[0], sems.at[1],
                device_id={"tile": peer}, device_id_type=MESH).start()

    def wait_units(ref, count, sem):
        some = pl.ds(0, count)
        pltpu.make_async_copy(ref.at[some], ref.at[some], sem).wait()

    @pl.when(owner)
    def _():
        near_ref[tile] = unit_at(flat_ref, unit)[...]
        wait_units(near_ref, PLANE - 1, sems.at[1])
        wait_units(near_ref, UNITS - 1, sems.at[0])
        near = jnp.sum(near_ref[...].astype(F32), axis=0).astype(BF)
        far_out_ref[0] = near
        far_ref[me] = near

        @pl.loop(1, SLIDES)
        def _(j):
            pltpu.make_async_remote_copy(
                far_out_ref.at[0], far_ref.at[me], sems.at[2], sems.at[3],
                device_id={"slide": shift(me, j, SLIDES)}, device_id_type=MESH).start()

        wait_units(far_ref, SLIDES - 1, sems.at[3])
        far_out_ref[1] = jnp.sum(far_ref[...].astype(F32), axis=0).astype(BF)
        pltpu.make_async_copy(far_out_ref.at[1], unit_at(res_ref, unit), sems.at[5]).start()

        @pl.loop(1, PLANE)
        def _(j):
            pltpu.make_async_remote_copy(
                far_out_ref.at[1], unit_at(res_ref, unit), sems.at[4], sems.at[5],
                device_id={"tile": shift(tile, j, PLANE)}, device_id_type=MESH).start()

        wait_units(far_ref, SLIDES - 1, sems.at[2])
        wait_units(near_ref, PLANE - 1, sems.at[4])

    @pl.when(jnp.logical_not(owner))
    def _():
        wait_units(near_ref, UNITS, sems.at[0])

    pltpu.make_async_copy(res_ref, res_ref, sems.at[5]).wait()


def step_kernel(
    maps_ref, dw_ref, bias_ref, gain_ref, win_hbm, wq_ref, seg_ref, dil_ref, slot_ref, len_ref, cot_ref,
    attn_ref, sums_ref,
    rows_ref, xt_ref, cv_ref, inv_ref, wb_ref, win_ref, w3_ref,
    out_ref, in_ref, back_out_ref, back_in_ref,
    pick_ref, cot_out_ref, cot_in_ref, blocks_ref, part_out_ref, part_in_ref, mixed_out_ref, mixed_in_ref,
    part_ref, flat_ref, near_ref, far_ref, far_out_ref, res_ref,
    local_sems, weight_send, weight_recv, share_sems, member_sems, route_sems, sum_sems,
):
    greet()
    for r in range(SIDE):
        map_copy(maps_ref, rows_ref, local_sems, r).start()
    win_copy = pltpu.make_async_copy(win_hbm, win_ref, local_sems.at[SIDE])
    win_copy.start()
    weights = Weights(w3_ref, weight_send, weight_recv, share_sems)
    member = weights.member
    pick_ref[...] = member_columns()
    cots = dot(cot_ref[...], pick_ref[...])
    cut = jnp.full((ROWS, LANE), len_ref[0, 0], jnp.int32).astype(F32)
    spare = iota((ROWS, LANE), 1) >= COLS
    for m in range(MEMBERS):
        cot_out_ref[m] = jnp.where(spare, cut, cots[:, m * LANE : (m + 1) * LANE]).astype(BF)
    spread_taps(dw_ref, wb_ref)
    transpose_maps(maps_ref, rows_ref, local_sems, xt_ref)
    greeted()
    weights.start(wq_ref)
    members_start(cot_out_ref, cot_in_ref, member_sems, 0)

    @pl.loop(0, CHUNKS)
    def _(chunk):
        conv_chunk(chunk, xt_ref, wb_ref, bias_ref, cv_ref)

    total = normalise(cv_ref, inv_ref, (0, SIDE), jnp.zeros((ROWS, C), F32))
    gain = gain_ref[...].reshape(1, C)
    pooled = (total * gain * (1.0 / AREA)).astype(BF)
    win_copy.wait()
    embed = dot(pooled, win_ref[...]).astype(BF)

    select, slots = send_rows(slot_ref)
    packed = jnp.concatenate([spread(embed), slots], axis=0)
    out_ref[...] = dot(select, packed).astype(BF).reshape(SLIDES, PACK, LANE)
    exchange_start(out_ref, in_ref, route_sems.at[0], route_sems.at[1])
    weights.hand_on()
    spread_slots, mask = slot_spread(), head_mask()
    members_wait(cot_in_ref, member_sems, 0)
    upstream = cot_in_ref[...].reshape(WIDE, LANE)
    cut = upstream[:, COLS : COLS + 1].astype(F32).astype(jnp.int32)
    allowed = allowed_pairs(member, seg_ref, dil_ref, cut)
    exchange_wait(out_ref, in_ref, route_sems.at[0], route_sems.at[1])
    arrived = in_ref[...].reshape(SLIDES * PACK, LANE)
    place = place_rows(spread_slots, arrived)
    blocks_ref[member] = gather_chunks(dot_first(place, arrived).astype(BF))
    members_start(None, blocks_ref, member_sems, 1, True)
    weights.finish()
    members_wait(blocks_ref, member_sems, 1)
    mixed, partial = attention(
        blocks_ref[...].reshape(WIDE, C), upstream[:, :COLS], w3_ref, mask, allowed)
    part_out_ref[...] = partial.astype(BF).reshape(MEMBERS, ROWS, C)
    members_start(part_out_ref, part_in_ref, member_sems, 2)
    padded = jnp.concatenate([mixed, jnp.zeros((WIDE, LANE - COLS), F32)], axis=1)
    mixed_out_ref[...] = padded.astype(BF).reshape(MEMBERS, ROWS, LANE)
    members_start(mixed_out_ref, mixed_in_ref, member_sems, 3)
    members_wait(part_in_ref, member_sems, 2)
    dblock = jnp.sum(part_in_ref[...].astype(F32), axis=0).astype(BF)
    back_out_ref[...] = dot(place, spread(dblock)).astype(BF).reshape(SLIDES, PACK, LANE)
    exchange_start(back_out_ref, back_in_ref, route_sems.at[2], route_sems.at[3])
    members_wait(mixed_in_ref, member_sems, 3)
    every = jnp.concatenate([mixed_in_ref[m] for m in range(MEMBERS)], axis=1)
    attn_ref[...] = dot_last(every, pick_ref[...]).astype(BF)
    weights.end()
    exchange_wait(back_out_ref, back_in_ref, route_sems.at[2], route_sems.at[3])
    returned = back_in_ref[...].reshape(SLIDES * PACK, LANE)
    dembed = gather_chunks(dot_first(select[:, : CHUNKS * ROWS], returned).astype(BF))
    dpool = dot_last(dembed, win_ref[...])

    bias_grad = conv_grads(dpool, gain, cv_ref, inv_ref)
    part_ref[...] = jnp.zeros(part_ref.shape, F32)
    part_ref[49:50] = jnp.sum(bias_grad, axis=0, keepdims=True)
    part_ref[50:51] = jnp.sum(dpool * total, axis=0, keepdims=True) * (1.0 / AREA)

    @pl.loop(0, CHUNKS)
    def _(chunk):
        tap_grads(chunk, xt_ref, cv_ref, part_ref)

    flat_ref[...] = part_ref[...].astype(BF)
    reduce_all(flat_ref, near_ref, far_ref, res_ref, far_out_ref, sum_sems)
    sums_ref[...] = res_ref[...]


def finish_kernel(attn_ref, res_ref, out_ref, kernel_ref, norm_ref):
    out_ref[...] = attn_ref[...]
    result = res_ref[...].astype(F32)
    kernel_ref[...] = result[:49]
    norm_ref[...] = result[49:51]


VMEM_LIMIT = 60 * 1024 * 1024


def params(**extra):
    return pltpu.CompilerParams(vmem_limit_bytes=VMEM_LIMIT, **extra)


def vmem(count):
    return [pl.BlockSpec(memory_space=pltpu.VMEM)] * count


def smem(count):
    return [pl.BlockSpec(memory_space=pltpu.SMEM)] * count


def shape(*dims, kind=BF):
    return jax.ShapeDtypeStruct(dims, kind)


def body(
    tile_maps, dw_kernel, conv_bias, norm_gain, w_in, w_qkv, seg_len, dilation,
    tile_slot, slide_lengths, cotangent,
):
    dma = pltpu.SemaphoreType.DMA
    hbm = [pl.BlockSpec(memory_space=pl.ANY)]
    message = pltpu.VMEM((SLIDES, PACK, LANE), BF)
    wide = pltpu.VMEM((MEMBERS, ROWS, C), BF)
    narrow = pltpu.VMEM((MEMBERS, ROWS, LANE), BF)
    attn, sums = pl.pallas_call(
        step_kernel,
        out_shape=[shape(ROWS, C), shape(SUM_ROWS, C)],
        in_specs=hbm + vmem(3) + hbm + vmem(1) + smem(4) + vmem(1),
        out_specs=vmem(2),
        scratch_shapes=[
            pltpu.VMEM((SIDE, ROWS, SIDE, C), BF), pltpu.VMEM((SIDE, SIDE, ROWS, C), F32),
            pltpu.VMEM((AREA, ROWS, C), F32), pltpu.VMEM((AREA, ROWS, LANE), F32),
            pltpu.VMEM((49, 8, C), F32), pltpu.VMEM((C, C), BF),
            pltpu.VMEM((3, SHARE, HEAD, C), BF), message, message, message, message,
            pltpu.VMEM((C, MEMBERS * LANE), BF), narrow, narrow, wide, wide, wide, narrow, narrow,
            pltpu.VMEM((SUM_ROWS, C), F32), pltpu.VMEM((SUM_ROWS, C), BF),
            pltpu.VMEM((PLANE, 16, LANE), BF), pltpu.VMEM((SLIDES, 16, LANE), BF),
            pltpu.VMEM((2, 16, LANE), BF), pltpu.VMEM((SUM_ROWS, C), BF),
            dma((9,)), dma((16,)), dma((2,)), dma((7,)), dma((2, 4)), dma((4,)), dma((6,)),
        ],
        compiler_params=params(collective_id=1, has_side_effects=True),
    )(
        tile_maps, dw_kernel, conv_bias, norm_gain, w_in, w_qkv.T,
        seg_len, dilation, tile_slot, slide_lengths, cotangent,
    )
    return pl.pallas_call(
        finish_kernel,
        out_shape=[shape(ROWS, C), shape(49, C, kind=F32), shape(2, C, kind=F32)],
        in_specs=vmem(2),
        out_specs=vmem(3),
    )(attn, sums)


def solution(mesh):
    both = ("tile", "slide")
    in_specs = (
        P(both, None, None, None), P(), P(), P(), P(), P(None, "slide"), P(), P(),
        P(both), P(both, None), P(both, None),
    )
    out_specs = (P(both, None), P(), P())
    return jax.shard_map(body, mesh=mesh, in_specs=in_specs, out_specs=out_specs, check_vma=False)
```

```python
import jax
import jax.numpy as jnp
from jax import lax
from jax.experimental import pallas as pl
from jax.experimental.pallas import tpu as pltpu
from jax.sharding import PartitionSpec as P

NORM_EPS = 1e-06
MESH = pl.DeviceIdType.MESH
BF = jnp.bfloat16
F32 = jnp.float32

SIDE = 8
AREA = SIDE * SIDE
REACH = 3
TAPS = 7
ROWS = 16
C = 768
LANE = 128
CHUNKS = C // LANE
HEADS = 16
HEAD = 48
SLIDES = 16
PLANE = 32
QUOTA = 3
PACK = 32
MEMBERS = 8
SHARE = HEADS // MEMBERS
WIDE = MEMBERS * ROWS
COLS = SHARE * HEAD
UNITS = 24
SUM_ROWS = 64


def iota(shape, dim):
    return lax.broadcasted_iota(jnp.int32, shape, dim)


def dot(left, right):
    return jnp.dot(left, right, preferred_element_type=F32)


def dot_last(left, right):
    return lax.dot_general(left, right, (((1,), (1,)), ((), ())), preferred_element_type=F32)


def dot_first(left, right):
    return lax.dot_general(left, right, (((0,), (0,)), ((), ())), preferred_element_type=F32)


def spread(block):
    return jnp.concatenate([block[:, k * LANE : (k + 1) * LANE] for k in range(CHUNKS)], axis=0)


def gather_chunks(stack):
    return jnp.concatenate([stack[k * ROWS : (k + 1) * ROWS] for k in range(CHUNKS)], axis=1)


def row_span(offset):
    return max(0, -offset), min(SIDE, SIDE - offset)


def map_copy(maps_ref, rows_ref, sems, r):
    return pltpu.make_async_copy(maps_ref.at[:, r], rows_ref.at[r], sems.at[r])


def transpose_maps(maps_ref, rows_ref, sems, xt_ref):
    row, col = iota((128, 128), 0), iota((128, 128), 1)
    perm = ((row >> 4) == (col & 7)) & ((row & 15) == (col >> 3))
    perm = perm.astype(F32).astype(BF)
    for r in range(SIDE):
        map_copy(maps_ref, rows_ref, sems, r).wait()
        part = rows_ref[r].astype(F32).reshape(128, C).astype(BF)
        xt_ref[r] = dot(perm, part).reshape(SIDE, ROWS, C)


POINTS = 20


def points(a):
    u = [a[0] + a[6], a[1] + a[7] if len(a) > 7 else a[1]] + a[2:6]
    v = [a[0] - a[6], a[1] - a[7] if len(a) > 7 else a[1]] + a[2:6]
    p = [u[k] + u[k + 3] for k in range(3)]
    q = [u[k] - u[k + 3] for k in range(3)]
    c0, c1 = p[0] - p[2], p[1] - p[2]
    e0, e1 = q[0] - q[2], q[1] + q[2]
    g0, g1 = v[0] - v[2] + v[4], v[1] - v[3] + v[5]
    h0, h1, h2, h3 = v[0] - v[4], v[1] - v[5], v[2] + v[4], v[3] + v[5]
    s0, s1 = h0 + h2, h1 + h3
    return [
        p[0] + p[1] + p[2], c0, c1, c0 + c1, q[0] - q[1] + q[2], e0, e1, e0 + e1,
        g0, g1, g0 + g1, h0, h1, h0 + h1, h2, h3, h2 + h3, s0, s1, s0 + s1,
    ]


POINT_SCALE = [0.25] * 8 + [0.5] * 12


def coefficients(m):
    third = 1.0 / 3.0
    c0, c1 = m[1] - m[2], m[3] - m[1] - m[2] - m[2]
    p2 = (m[0] - c0 - c1) * third
    p = [c0 + p2, c1 + p2, p2]
    e0, e1 = m[5] - m[6], m[7] - m[5]
    q2 = (m[4] - e0 + e1) * third
    q = [e0 + q2, e1 - q2, q2]
    u = [p[k] + q[k] for k in range(3)] + [p[k] - q[k] for k in range(3)]
    g0, g1 = m[8] - m[9], m[10] - m[8] - m[9]
    a1, b1, s1 = m[13] - m[11] - m[12], m[16] - m[14] - m[15], m[19] - m[17] - m[18]
    s0, s2 = m[17] - m[11], m[18] - m[12]
    h0 = m[11] - m[14] - s2
    h1 = a1 - b1
    h2 = m[12] - m[15] + s0 + s2
    h3 = s1 - a1
    v4, v5 = (g0 - h0 + h2) * third, (g1 - h1 + h3) * third
    v = [h0 + v4, h1 + v5, h2 - v4, h3 - v5, v4, v5]
    return [u[k] + v[k] for k in (3, 4, 5)] + [u[k] - v[k] for k in range(5)]


def spread_taps(dw_ref, wb_ref):
    taps = dw_ref[...].astype(F32)
    for r in range(TAPS):
        row = [taps[r * TAPS + s : r * TAPS + s + 1] for s in range(TAPS)]
        for f, point in enumerate(points(row[::-1])):
            wb_ref[f, r] = jnp.broadcast_to(point * POINT_SCALE[f], (8, C))


def conv_chunk(chunk, xt_ref, xp_ref, yp_ref, wb_ref, bias_ref, cv_ref):
    lanes = pl.ds(pl.multiple_of(chunk * LANE, LANE), LANE)
    bias = jnp.broadcast_to(bias_ref[lanes].reshape(1, LANE), (ROWS, LANE))
    for i in range(SIDE):
        for f, point in enumerate(points([xt_ref[i, j, :, lanes] for j in range(SIDE)])):
            xp_ref[f, i, :, lanes] = point

    @pl.loop(0, POINTS)
    def _(f):
        cells = [xp_ref[f, i, :, lanes].reshape(2, 8, LANE) for i in range(SIDE)]
        taps = [wb_ref[f, r, :, lanes] for r in range(TAPS)]
        for i in range(SIDE):
            total = None
            for r in range(TAPS):
                if 0 <= i + r - REACH < SIDE:
                    term = cells[i + r - REACH] * taps[r]
                    total = term if total is None else total + term
            yp_ref[f, i] = total.reshape(ROWS, LANE)

    for i in range(SIDE):
        for j, value in enumerate(coefficients([yp_ref[f, i] for f in range(POINTS)])):
            cv_ref[i * SIDE + j, :, lanes] = value + bias


def normalise(cv_ref, inv_ref, rows, total):
    def step(b, total):
        some = pl.ds(b * SIDE, SIDE)
        mean = jnp.mean(cv_ref[some], axis=2, keepdims=True)
        centered = cv_ref[some] - mean
        inv = lax.rsqrt(jnp.mean(centered * centered, axis=2, keepdims=True) + NORM_EPS)
        normed = (cv_ref[some] - mean) * inv
        cv_ref[some] = normed
        inv_ref[some] = jnp.broadcast_to(inv, (SIDE, ROWS, LANE))
        return total + jnp.sum(normed, axis=0)

    return lax.fori_loop(rows[0], rows[1], step, total)


def send_rows(slot_ref):
    lane = iota((1, 112), 1)
    tile, chunk = lane & 15, lane >> 4
    owner = jnp.zeros((1, 112), jnp.int32)
    for t in range(ROWS):
        owner = jnp.where(tile == t, slot_ref[t] >> 4, owner)
    rank = jnp.zeros((1, 112), jnp.int32)
    for t in range(ROWS):
        rank = rank + jnp.where((owner == (slot_ref[t] >> 4)) & (tile > t), 1, 0)
    want = owner * PACK + chunk * QUOTA + rank
    select = (iota((SLIDES * PACK, 112), 0) == want).astype(F32).astype(BF)
    sub = iota((ROWS, LANE), 0)
    slots = jnp.zeros((ROWS, LANE), jnp.int32)
    for t in range(ROWS):
        slots = jnp.where(sub == t, (slot_ref[t] & 15) + 1, slots)
    return select, slots.astype(F32).astype(BF)


def slot_spread():
    size = SLIDES * PACK
    row, col = iota((size, size), 0), iota((size, size), 1)
    inside = row & (PACK - 1)
    quota = inside
    for k in range(1, PACK // QUOTA + 1):
        quota = jnp.where(inside >= k * QUOTA, inside - k * QUOTA, quota)
    return (col == (row - inside + CHUNKS * QUOTA + quota)).astype(F32).astype(BF)


def place_rows(spread_slots, arrived):
    size = SLIDES * PACK
    slot = dot(spread_slots, arrived)[:, : CHUNKS * ROWS]
    inside = iota((size, CHUNKS * ROWS), 0) & (PACK - 1)
    lane = iota((size, CHUNKS * ROWS), 1)
    first = (lane >> 4) * QUOTA
    want = ((lane & 15) + 1).astype(F32)
    hit = (inside >= first) & (inside < first + QUOTA) & (slot == want)
    return hit.astype(F32).astype(BF)


def head_mask():
    row, lane = iota((SHARE * WIDE, COLS), 0), iota((SHARE * WIDE, COLS), 1)
    low = jnp.where(row >= WIDE, HEAD, 0)
    return ((lane >= low) & (lane < low + HEAD)).astype(F32).astype(BF)


def member_columns():
    row, col = iota((C, MEMBERS * LANE), 0), iota((C, MEMBERS * LANE), 1)
    lane = col & (LANE - 1)
    first = (col >> 7) * HEAD + lane
    want = jnp.where(lane < HEAD, first, first + (MEMBERS - 1) * HEAD)
    want = jnp.where(lane < COLS, want, -1)
    return (row == want).astype(F32).astype(BF)


def allowed_pairs(member, seg_ref, dil_ref, cut):
    left, right = iota((WIDE, WIDE), 0), iota((WIDE, WIDE), 1)
    slot_left, slot_right = left & 15, right & 15
    run_left, run_right = slot_left >= cut, slot_right >= cut
    pos_left = jnp.where(run_left, slot_left - cut, slot_left)
    pos_right = jnp.where(run_right, slot_right - cut, slot_right)
    apart = pos_left ^ pos_right
    apart = jnp.where(run_left != run_right, apart | 256, apart)
    apart = jnp.where((left >> 4) != (right >> 4), apart | 256, apart)
    parts = []
    for h in range(SHARE):
        seg, dil = seg_ref[member + MEMBERS * h], dil_ref[member + MEMBERS * h]
        parts.append(apart & (~(seg - 1) | (dil - 1)))
    return jnp.concatenate(parts, axis=0) == 0


def attention(block, upstream, w3_ref, mask, allowed):
    scale = HEAD ** (-0.5)
    weights = [w3_ref[part].reshape(COLS, C) for part in range(3)]
    query, key, value = [dot_last(block, each).astype(BF) for each in weights]
    many_query = jnp.concatenate([query] * SHARE, axis=0) * mask
    many_grad = jnp.concatenate([upstream] * SHARE, axis=0) * mask
    scores = dot_last(many_query, key) * scale
    masked = jnp.where(allowed, scores, -1e30)
    top = jnp.max(masked, axis=1, keepdims=True)
    expo = jnp.where(allowed, jnp.exp(masked - top), 0.0)
    prob = expo / jnp.sum(expo, axis=1, keepdims=True)
    prob_bf = prob.astype(BF)
    mask_f = mask.astype(F32)

    def own_head(full):
        return jnp.sum((full * mask_f).reshape(SHARE, WIDE, COLS), axis=0)

    mixed = own_head(dot(prob_bf, value))
    dprob = dot_last(many_grad, value)
    dscore = (prob * (dprob - jnp.sum(prob * dprob, axis=1, keepdims=True)) * scale).astype(BF)
    dquery = own_head(dot(dscore, key)).astype(BF)
    dkey = dot_first(dscore, many_query).astype(BF)
    dvalue = dot_first(prob_bf, many_grad).astype(BF)
    total = dot(dquery, weights[0]) + dot(dkey, weights[1]) + dot(dvalue, weights[2])
    return mixed, total


def shift(index, by, size):
    return (index + by + size) & (size - 1)


class Weights:
    def __init__(self, w3_ref, send_sems, recv_sems, share_sems):
        self.w3_ref, self.send, self.recv, self.share = w3_ref, send_sems, recv_sems, share_sems
        self.tile, self.me = lax.axis_index("tile"), lax.axis_index("slide")
        self.y = (self.tile >> 1) & 3
        self.member = (self.tile >> 3) * 2 + (self.tile & 1)
        self.carrier = self.y < 3
        self.row = pl.multiple_of(jnp.minimum(self.y, 2) * 16, 16)
        self.source = self.carrier & ((self.me & 7) == self.member)

    def along_z(self, j):
        head = self.me >> 3
        rows = self.w3_ref.at[:, head, pl.ds(self.row, 16)]
        return pltpu.make_async_remote_copy(
            rows, rows, self.send.at[j], self.recv.at[head],
            device_id={"slide": shift(self.me, j, SLIDES)}, device_id_type=MESH)

    def along_y(self, j):
        peer = (self.tile & ~6) | (((self.y + j) & 3) << 1)
        rows = self.w3_ref.at[:, :, pl.ds(self.row, 16)]
        return pltpu.make_async_remote_copy(
            rows, rows, self.share.at[3 + j], self.share.at[jnp.minimum(self.y, 2)],
            device_id={"tile": peer}, device_id_type=MESH)

    def start(self, wq_ref):
        @pl.when(self.source)
        def _():
            for part in range(3):
                self.w3_ref[part, self.me >> 3, pl.ds(self.row, 16)] = wq_ref[
                    pl.ds(pl.multiple_of(part * HEAD + self.row, 16), 16)]

            @pl.loop(1, SLIDES)
            def _(j):
                self.along_z(j).start()

    def hand_on(self):
        @pl.when(self.carrier)
        def _():
            for head in range(SHARE):

                @pl.when(self.me != self.member + MEMBERS * head)
                def _():
                    rows = self.w3_ref.at[:, head, pl.ds(0, 16)]
                    pltpu.make_async_copy(rows, rows, self.recv.at[head]).wait()

            for j in range(1, 4):
                self.along_y(j).start()

    def finish(self):
        for y in range(3):

            @pl.when(self.y != y)
            def _():
                rows = self.w3_ref.at[:, :, pl.ds(16 * y, 16)]
                pltpu.make_async_copy(rows, rows, self.share.at[y]).wait()

    def end(self):
        @pl.when(self.source)
        def _():
            @pl.loop(1, SLIDES)
            def _(j):
                self.along_z(j).wait_send()

        @pl.when(self.carrier)
        def _():
            for j in range(1, 4):
                self.along_y(j).wait_send()


def members_start(out_ref, in_ref, sems, n, same=False):
    tile = lax.axis_index("tile")
    member = (tile >> 3) * 2 + (tile & 1)
    if not same:
        in_ref[member] = out_ref[member]

    @pl.loop(1, MEMBERS)
    def _(j):
        peer = shift(member, j, MEMBERS)
        pltpu.make_async_remote_copy(
            in_ref.at[member] if same else out_ref.at[peer], in_ref.at[member],
            sems.at[0, n], sems.at[1, n],
            device_id={"tile": (peer >> 1) * 8 + (tile & 6) + (peer & 1)}, device_id_type=MESH).start()


def members_wait(in_ref, sems, n):
    some = in_ref.at[pl.ds(0, MEMBERS - 1)]
    pltpu.make_async_copy(some, some, sems.at[1, n]).wait()
    pltpu.make_async_copy(some, some, sems.at[0, n]).wait()


def exchange_start(out_ref, in_ref, send_sem, recv_sem):
    me = lax.axis_index("slide")
    in_ref[me] = out_ref[me]

    @pl.loop(1, SLIDES)
    def _(j):
        peer = shift(me, j, SLIDES)
        pltpu.make_async_remote_copy(
            out_ref.at[peer], in_ref.at[me], send_sem, recv_sem,
            device_id={"slide": peer}, device_id_type=MESH).start()


def exchange_wait(out_ref, in_ref, send_sem, recv_sem):
    some = pl.ds(0, SLIDES - 1)
    pltpu.make_async_copy(in_ref.at[some], in_ref.at[some], recv_sem).wait()
    pltpu.make_async_copy(out_ref.at[some], out_ref.at[some], send_sem).wait()


def greet():
    tile, me = lax.axis_index("tile"), lax.axis_index("slide")
    barrier = pltpu.get_barrier_semaphore()

    @pl.loop(1, SLIDES)
    def _(j):
        pl.semaphore_signal(
            barrier, inc=1, device_id={"slide": shift(me, j, SLIDES)}, device_id_type=MESH)

    @pl.loop(1, PLANE)
    def _(j):
        pl.semaphore_signal(
            barrier, inc=1, device_id={"tile": shift(tile, j, PLANE)}, device_id_type=MESH)


def greeted():
    pl.semaphore_wait(pltpu.get_barrier_semaphore(), SLIDES + PLANE - 2)


def conv_grads(dpool, gain, cv_ref, inv_ref):
    grad = dpool * (gain * (1.0 / AREA))
    level = grad - jnp.mean(grad, axis=1, keepdims=True)

    def step(b, total):
        some = pl.ds(b * SIDE, SIDE)
        along = jnp.mean(cv_ref[some] * grad, axis=2, keepdims=True)
        dconv = inv_ref[some][:, :, :1] * (level - cv_ref[some] * along)
        cv_ref[some] = dconv
        return total + jnp.sum(dconv, axis=0)

    return lax.fori_loop(0, SIDE, step, jnp.zeros((ROWS, C), F32))


def tap_grads(chunk, xp_ref, yp_ref, cv_ref, sp_ref):
    lanes = pl.ds(pl.multiple_of(chunk * LANE, LANE), LANE)
    for i in range(SIDE):
        row = [cv_ref[i * SIDE + j, :, lanes] for j in range(SIDE)]
        for f, point in enumerate(points(row[::-1])):
            yp_ref[f, i] = point

    @pl.loop(0, POINTS)
    def _(f):
        cells = [xp_ref[f, i, :, lanes] for i in range(SIDE)]
        grads = [yp_ref[f, i] for i in range(SIDE)]
        for r in range(TAPS):
            total = None
            for i in range(*row_span(r - REACH)):
                term = cells[i + r - REACH] * grads[i]
                total = term if total is None else total + term
            sp_ref[f, r : r + 1] = jnp.sum(total, axis=0, keepdims=True)

    return coefficients([sp_ref[f] * POINT_SCALE[f] for f in range(POINTS)])[1:]


def unit_at(ref, unit):
    rows = pl.ds(pl.multiple_of((unit & 3) * 16, 16), 16)
    lanes = pl.ds(pl.multiple_of((unit >> 2) * LANE, LANE), LANE)
    return ref.at[rows, lanes]


def owner_of(unit):
    return unit + ((unit * 11) >> 5)


def send_chunk(chunk, flat_ref, near_ref, sems):
    tile = lax.axis_index("tile")
    for rows in range(4):
        unit = chunk * 4 + rows
        peer = owner_of(unit)

        @pl.when(peer != tile)
        def _():
            pltpu.make_async_remote_copy(
                unit_at(flat_ref, unit), near_ref.at[tile], sems.at[0], sems.at[1],
                device_id={"tile": peer}, device_id_type=MESH).start()


def reduce_all(flat_ref, near_ref, far_ref, res_ref, far_out_ref, sems):
    tile, me = lax.axis_index("tile"), lax.axis_index("slide")
    owner = (tile & 3) != 3
    unit = jnp.minimum((tile >> 2) * 3 + (tile & 3), UNITS - 1)

    def wait_units(ref, count, sem):
        some = pl.ds(0, count)
        pltpu.make_async_copy(ref.at[some], ref.at[some], sem).wait()

    @pl.when(owner)
    def _():
        near_ref[tile] = unit_at(flat_ref, unit)[...]
        wait_units(near_ref, PLANE - 1, sems.at[1])
        wait_units(near_ref, UNITS - 1, sems.at[0])
        near = jnp.sum(near_ref[...].astype(F32), axis=0).astype(BF)
        far_out_ref[0] = near
        far_ref[me] = near

        @pl.loop(1, SLIDES)
        def _(j):
            pltpu.make_async_remote_copy(
                far_out_ref.at[0], far_ref.at[me], sems.at[2], sems.at[3],
                device_id={"slide": shift(me, j, SLIDES)}, device_id_type=MESH).start()

        wait_units(far_ref, SLIDES - 1, sems.at[3])
        far_out_ref[1] = jnp.sum(far_ref[...].astype(F32), axis=0).astype(BF)
        pltpu.make_async_copy(far_out_ref.at[1], unit_at(res_ref, unit), sems.at[5]).start()

        @pl.loop(1, PLANE)
        def _(j):
            pltpu.make_async_remote_copy(
                far_out_ref.at[1], unit_at(res_ref, unit), sems.at[4], sems.at[5],
                device_id={"tile": shift(tile, j, PLANE)}, device_id_type=MESH).start()

        wait_units(far_ref, SLIDES - 1, sems.at[2])
        wait_units(near_ref, PLANE - 1, sems.at[4])

    @pl.when(jnp.logical_not(owner))
    def _():
        wait_units(near_ref, UNITS, sems.at[0])

    pltpu.make_async_copy(res_ref, res_ref, sems.at[5]).wait()


def step_kernel(
    maps_ref, dw_ref, bias_ref, gain_ref, win_hbm, wq_ref, seg_ref, dil_ref, slot_ref, len_ref, cot_ref,
    attn_ref, sums_ref,
    rows_ref, xt_ref, cv_ref, inv_ref, wb_ref, win_ref, w3_ref,
    out_ref, in_ref, back_out_ref, back_in_ref,
    pick_ref, cot_out_ref, cot_in_ref, blocks_ref, part_out_ref, part_in_ref, mixed_out_ref, mixed_in_ref,
    xp_ref, yp_ref, sp_ref, norm_ref, flat_ref, near_ref, far_ref, far_out_ref, res_ref,
    local_sems, weight_send, weight_recv, share_sems, member_sems, route_sems, sum_sems,
):
    greet()
    for r in range(SIDE):
        map_copy(maps_ref, rows_ref, local_sems, r).start()
    win_copy = pltpu.make_async_copy(win_hbm, win_ref, local_sems.at[SIDE])
    win_copy.start()
    weights = Weights(w3_ref, weight_send, weight_recv, share_sems)
    member = weights.member
    pick_ref[...] = member_columns()
    cots = dot(cot_ref[...], pick_ref[...])
    cut = jnp.full((ROWS, LANE), len_ref[0, 0], jnp.int32).astype(F32)
    spare = iota((ROWS, LANE), 1) >= COLS
    for m in range(MEMBERS):
        cot_out_ref[m] = jnp.where(spare, cut, cots[:, m * LANE : (m + 1) * LANE]).astype(BF)
    spread_taps(dw_ref, wb_ref)
    transpose_maps(maps_ref, rows_ref, local_sems, xt_ref)
    greeted()
    weights.start(wq_ref)
    members_start(cot_out_ref, cot_in_ref, member_sems, 0)

    @pl.loop(0, CHUNKS)
    def _(chunk):
        conv_chunk(chunk, xt_ref, xp_ref, yp_ref, wb_ref, bias_ref, cv_ref)

    total = normalise(cv_ref, inv_ref, (0, SIDE), jnp.zeros((ROWS, C), F32))
    gain = gain_ref[...].reshape(1, C)
    pooled = (total * gain * (1.0 / AREA)).astype(BF)
    win_copy.wait()
    embed = dot(pooled, win_ref[...]).astype(BF)

    select, slots = send_rows(slot_ref)
    packed = jnp.concatenate([spread(embed), slots], axis=0)
    out_ref[...] = dot(select, packed).astype(BF).reshape(SLIDES, PACK, LANE)
    exchange_start(out_ref, in_ref, route_sems.at[0], route_sems.at[1])
    weights.hand_on()
    spread_slots, mask = slot_spread(), head_mask()
    members_wait(cot_in_ref, member_sems, 0)
    upstream = cot_in_ref[...].reshape(WIDE, LANE)
    cut = upstream[:, COLS : COLS + 1].astype(F32).astype(jnp.int32)
    allowed = allowed_pairs(member, seg_ref, dil_ref, cut)
    exchange_wait(out_ref, in_ref, route_sems.at[0], route_sems.at[1])
    arrived = in_ref[...].reshape(SLIDES * PACK, LANE)
    place = place_rows(spread_slots, arrived)
    blocks_ref[member] = gather_chunks(dot_first(place, arrived).astype(BF))
    members_start(None, blocks_ref, member_sems, 1, True)
    weights.finish()
    members_wait(blocks_ref, member_sems, 1)
    mixed, partial = attention(
        blocks_ref[...].reshape(WIDE, C), upstream[:, :COLS], w3_ref, mask, allowed)
    part_out_ref[...] = partial.astype(BF).reshape(MEMBERS, ROWS, C)
    members_start(part_out_ref, part_in_ref, member_sems, 2)
    padded = jnp.concatenate([mixed, jnp.zeros((WIDE, LANE - COLS), F32)], axis=1)
    mixed_out_ref[...] = padded.astype(BF).reshape(MEMBERS, ROWS, LANE)
    members_start(mixed_out_ref, mixed_in_ref, member_sems, 3)
    members_wait(part_in_ref, member_sems, 2)
    dblock = jnp.sum(part_in_ref[...].astype(F32), axis=0).astype(BF)
    back_out_ref[...] = dot(place, spread(dblock)).astype(BF).reshape(SLIDES, PACK, LANE)
    exchange_start(back_out_ref, back_in_ref, route_sems.at[2], route_sems.at[3])
    members_wait(mixed_in_ref, member_sems, 3)
    every = jnp.concatenate([mixed_in_ref[m] for m in range(MEMBERS)], axis=1)
    attn_ref[...] = dot_last(every, pick_ref[...]).astype(BF)
    weights.end()
    exchange_wait(back_out_ref, back_in_ref, route_sems.at[2], route_sems.at[3])
    returned = back_in_ref[...].reshape(SLIDES * PACK, LANE)
    dembed = gather_chunks(dot_first(select[:, : CHUNKS * ROWS], returned).astype(BF))
    dpool = dot_last(dembed, win_ref[...])

    bias_grad = conv_grads(dpool, gain, cv_ref, inv_ref)
    norm_ref[0:1] = jnp.sum(bias_grad, axis=0, keepdims=True)
    norm_ref[1:2] = jnp.sum(dpool * total, axis=0, keepdims=True) * (1.0 / AREA)
    sp_ref[...] = jnp.zeros(sp_ref.shape, F32)

    @pl.loop(0, CHUNKS)
    def _(chunk):
        lanes = pl.ds(pl.multiple_of(chunk * LANE, LANE), LANE)
        blocks = tap_grads(chunk, xp_ref, yp_ref, cv_ref, sp_ref)
        last = iota((8, LANE), 0) == TAPS
        for k in range(2):
            blocks[k] = jnp.where(last, norm_ref[k : k + 1, lanes], blocks[k])
        blocks.append(jnp.zeros((8, LANE), F32))
        flat_ref[:, lanes] = jnp.concatenate(blocks, axis=0).astype(BF)
        send_chunk(chunk, flat_ref, near_ref, sum_sems)

    reduce_all(flat_ref, near_ref, far_ref, res_ref, far_out_ref, sum_sems)
    sums_ref[...] = res_ref[...]


def finish_kernel(attn_ref, res_ref, out_ref, kernel_ref, norm_ref):
    out_ref[...] = attn_ref[...]
    result = res_ref[...].astype(F32)
    for r in range(TAPS):
        for s in range(TAPS):
            kernel_ref[r * TAPS + s : r * TAPS + s + 1] = result[s * 8 + r : s * 8 + r + 1]
    for k in range(2):
        norm_ref[k : k + 1] = result[k * 8 + TAPS : k * 8 + TAPS + 1]


VMEM_LIMIT = 60 * 1024 * 1024


def params(**extra):
    return pltpu.CompilerParams(vmem_limit_bytes=VMEM_LIMIT, **extra)


def vmem(count):
    return [pl.BlockSpec(memory_space=pltpu.VMEM)] * count


def smem(count):
    return [pl.BlockSpec(memory_space=pltpu.SMEM)] * count


def shape(*dims, kind=BF):
    return jax.ShapeDtypeStruct(dims, kind)


def body(
    tile_maps, dw_kernel, conv_bias, norm_gain, w_in, w_qkv, seg_len, dilation,
    tile_slot, slide_lengths, cotangent,
):
    dma = pltpu.SemaphoreType.DMA
    hbm = [pl.BlockSpec(memory_space=pl.ANY)]
    message = pltpu.VMEM((SLIDES, PACK, LANE), BF)
    wide = pltpu.VMEM((MEMBERS, ROWS, C), BF)
    narrow = pltpu.VMEM((MEMBERS, ROWS, LANE), BF)
    attn, sums = pl.pallas_call(
        step_kernel,
        out_shape=[shape(ROWS, C), shape(SUM_ROWS, C)],
        in_specs=hbm + vmem(3) + hbm + vmem(1) + smem(4) + vmem(1),
        out_specs=vmem(2),
        scratch_shapes=[
            pltpu.VMEM((SIDE, ROWS, SIDE, C), BF), pltpu.VMEM((SIDE, SIDE, ROWS, C), F32),
            pltpu.VMEM((AREA, ROWS, C), F32), pltpu.VMEM((AREA, ROWS, LANE), F32),
            pltpu.VMEM((POINTS, TAPS, 8, C), F32), pltpu.VMEM((C, C), BF),
            pltpu.VMEM((3, SHARE, HEAD, C), BF), message, message, message, message,
            pltpu.VMEM((C, MEMBERS * LANE), BF), narrow, narrow, wide, wide, wide, narrow, narrow,
            pltpu.VMEM((POINTS, SIDE, ROWS, C), F32), pltpu.VMEM((POINTS, SIDE, ROWS, LANE), F32),
            pltpu.VMEM((POINTS, 8, LANE), F32), pltpu.VMEM((2, C), F32), pltpu.VMEM((SUM_ROWS, C), BF),
            pltpu.VMEM((PLANE, 16, LANE), BF), pltpu.VMEM((SLIDES, 16, LANE), BF),
            pltpu.VMEM((2, 16, LANE), BF), pltpu.VMEM((SUM_ROWS, C), BF),
            dma((9,)), dma((16,)), dma((2,)), dma((7,)), dma((2, 4)), dma((4,)), dma((6,)),
        ],
        compiler_params=params(collective_id=1, has_side_effects=True),
    )(
        tile_maps, dw_kernel, conv_bias, norm_gain, w_in, w_qkv.T,
        seg_len, dilation, tile_slot, slide_lengths, cotangent,
    )
    return pl.pallas_call(
        finish_kernel,
        out_shape=[shape(ROWS, C), shape(49, C, kind=F32), shape(2, C, kind=F32)],
        in_specs=vmem(2),
        out_specs=vmem(3),
    )(attn, sums)


def solution(mesh):
    both = ("tile", "slide")
    in_specs = (
        P(both, None, None, None), P(), P(), P(), P(), P(None, "slide"), P(), P(),
        P(both), P(both, None), P(both, None),
    )
    out_specs = (P(both, None), P(), P())
    return jax.shard_map(body, mesh=mesh, in_specs=in_specs, out_specs=out_specs, check_vma=False)
```

```python
import jax
import jax.numpy as jnp
from jax import lax
from jax.experimental import pallas as pl
from jax.experimental.pallas import tpu as pltpu
from jax.sharding import PartitionSpec as P

NORM_EPS = 1e-06
MESH = pl.DeviceIdType.MESH
BF = jnp.bfloat16
F32 = jnp.float32

SIDE = 8
AREA = SIDE * SIDE
REACH = 3
TAPS = 7
ROWS = 16
C = 768
LANE = 128
CHUNKS = C // LANE
HEADS = 16
HEAD = 48
SLIDES = 16
PLANE = 32
QUOTA = 3
PACK = 32
MEMBERS = 8
SHARE = HEADS // MEMBERS
WIDE = MEMBERS * ROWS
COLS = SHARE * HEAD
UNITS = 24
SUM_ROWS = 64


def iota(shape, dim):
    return lax.broadcasted_iota(jnp.int32, shape, dim)


def dot(left, right):
    return jnp.dot(left, right, preferred_element_type=F32)


def dot_last(left, right):
    return lax.dot_general(left, right, (((1,), (1,)), ((), ())), preferred_element_type=F32)


def dot_first(left, right):
    return lax.dot_general(left, right, (((0,), (0,)), ((), ())), preferred_element_type=F32)


def spread(block):
    return jnp.concatenate([block[:, k * LANE : (k + 1) * LANE] for k in range(CHUNKS)], axis=0)


def gather_chunks(stack):
    return jnp.concatenate([stack[k * ROWS : (k + 1) * ROWS] for k in range(CHUNKS)], axis=1)


def row_span(offset):
    return max(0, -offset), min(SIDE, SIDE - offset)


def map_copy(maps_ref, rows_ref, sems, r):
    return pltpu.make_async_copy(maps_ref.at[:, r], rows_ref.at[r], sems.at[r])


def transpose_maps(maps_ref, rows_ref, sems, xt_ref):
    row, col = iota((128, 128), 0), iota((128, 128), 1)
    perm = ((row >> 4) == (col & 7)) & ((row & 15) == (col >> 3))
    perm = perm.astype(F32).astype(BF)
    for r in range(SIDE):
        map_copy(maps_ref, rows_ref, sems, r).wait()
        part = rows_ref[r].astype(F32).reshape(128, C).astype(BF)
        xt_ref[r] = dot(perm, part).reshape(SIDE, ROWS, C)


POINTS = 20


def points(a):
    u = [a[0] + a[6], a[1] + a[7] if len(a) > 7 else a[1]] + a[2:6]
    v = [a[0] - a[6], a[1] - a[7] if len(a) > 7 else a[1]] + a[2:6]
    p = [u[k] + u[k + 3] for k in range(3)]
    q = [u[k] - u[k + 3] for k in range(3)]
    c0, c1 = p[0] - p[2], p[1] - p[2]
    e0, e1 = q[0] - q[2], q[1] + q[2]
    g0, g1 = v[0] - v[2] + v[4], v[1] - v[3] + v[5]
    h0, h1, h2, h3 = v[0] - v[4], v[1] - v[5], v[2] + v[4], v[3] + v[5]
    s0, s1 = h0 + h2, h1 + h3
    return [
        p[0] + p[1] + p[2], c0, c1, c0 + c1, q[0] - q[1] + q[2], e0, e1, e0 + e1,
        g0, g1, g0 + g1, h0, h1, h0 + h1, h2, h3, h2 + h3, s0, s1, s0 + s1,
    ]


POINT_SCALE = [0.25] * 8 + [0.5] * 12


def coefficients(m):
    third = 1.0 / 3.0
    c0, c1 = m[1] - m[2], m[3] - m[1] - m[2] - m[2]
    p2 = (m[0] - c0 - c1) * third
    p = [c0 + p2, c1 + p2, p2]
    e0, e1 = m[5] - m[6], m[7] - m[5]
    q2 = (m[4] - e0 + e1) * third
    q = [e0 + q2, e1 - q2, q2]
    u = [p[k] + q[k] for k in range(3)] + [p[k] - q[k] for k in range(3)]
    g0, g1 = m[8] - m[9], m[10] - m[8] - m[9]
    a1, b1, s1 = m[13] - m[11] - m[12], m[16] - m[14] - m[15], m[19] - m[17] - m[18]
    s0, s2 = m[17] - m[11], m[18] - m[12]
    h0 = m[11] - m[14] - s2
    h1 = a1 - b1
    h2 = m[12] - m[15] + s0 + s2
    h3 = s1 - a1
    v4, v5 = (g0 - h0 + h2) * third, (g1 - h1 + h3) * third
    v = [h0 + v4, h1 + v5, h2 - v4, h3 - v5, v4, v5]
    return [u[k] + v[k] for k in (3, 4, 5)] + [u[k] - v[k] for k in range(5)]


def spread_taps(dw_ref, wb_ref):
    taps = dw_ref[...].astype(F32)
    for r in range(TAPS):
        row = [taps[r * TAPS + s : r * TAPS + s + 1] for s in range(TAPS)]
        for f, point in enumerate(points(row[::-1])):
            wb_ref[f, r] = jnp.broadcast_to(point * POINT_SCALE[f], (8, C))


def conv_chunk(chunk, xt_ref, xp_ref, yp_ref, wb_ref, bias_ref, cv_ref):
    lanes = pl.ds(pl.multiple_of(chunk * LANE, LANE), LANE)
    bias = jnp.broadcast_to(bias_ref[lanes].reshape(1, LANE), (ROWS, LANE))
    for i in range(SIDE):
        for f, point in enumerate(points([xt_ref[i, j, :, lanes] for j in range(SIDE)])):
            xp_ref[f, i, :, lanes] = point

    @pl.loop(0, POINTS, unroll=5)
    def _(f):
        cells = [xp_ref[f, i, :, lanes].reshape(2, 8, LANE) for i in range(SIDE)]
        taps = [wb_ref[f, r, :, lanes] for r in range(TAPS)]
        for i in range(SIDE):
            total = None
            for r in range(TAPS):
                if 0 <= i + r - REACH < SIDE:
                    term = cells[i + r - REACH] * taps[r]
                    total = term if total is None else total + term
            yp_ref[f, i] = total.reshape(ROWS, LANE)

    for i in range(SIDE):
        for j, value in enumerate(coefficients([yp_ref[f, i] for f in range(POINTS)])):
            cv_ref[i * SIDE + j, :, lanes] = value + bias


def normalise(cv_ref, inv_ref, rows, total):
    def step(b, total):
        some = pl.ds(b * SIDE, SIDE)
        mean = jnp.mean(cv_ref[some], axis=2, keepdims=True)
        centered = cv_ref[some] - mean
        inv = lax.rsqrt(jnp.mean(centered * centered, axis=2, keepdims=True) + NORM_EPS)
        normed = (cv_ref[some] - mean) * inv
        cv_ref[some] = normed
        inv_ref[some] = jnp.broadcast_to(inv, (SIDE, ROWS, LANE))
        return total + jnp.sum(normed, axis=0)

    return lax.fori_loop(rows[0], rows[1], step, total)


def send_rows(slot_ref):
    lane = iota((1, 112), 1)
    tile, chunk = lane & 15, lane >> 4
    owner = jnp.zeros((1, 112), jnp.int32)
    for t in range(ROWS):
        owner = jnp.where(tile == t, slot_ref[t] >> 4, owner)
    rank = jnp.zeros((1, 112), jnp.int32)
    for t in range(ROWS):
        rank = rank + jnp.where((owner == (slot_ref[t] >> 4)) & (tile > t), 1, 0)
    want = owner * PACK + chunk * QUOTA + rank
    select = (iota((SLIDES * PACK, 112), 0) == want).astype(F32).astype(BF)
    sub = iota((ROWS, LANE), 0)
    slots = jnp.zeros((ROWS, LANE), jnp.int32)
    for t in range(ROWS):
        slots = jnp.where(sub == t, (slot_ref[t] & 15) + 1, slots)
    return select, slots.astype(F32).astype(BF)


def slot_spread():
    size = SLIDES * PACK
    row, col = iota((size, size), 0), iota((size, size), 1)
    inside = row & (PACK - 1)
    quota = inside
    for k in range(1, PACK // QUOTA + 1):
        quota = jnp.where(inside >= k * QUOTA, inside - k * QUOTA, quota)
    return (col == (row - inside + CHUNKS * QUOTA + quota)).astype(F32).astype(BF)


def place_rows(spread_slots, arrived):
    size = SLIDES * PACK
    slot = dot(spread_slots, arrived)[:, : CHUNKS * ROWS]
    inside = iota((size, CHUNKS * ROWS), 0) & (PACK - 1)
    lane = iota((size, CHUNKS * ROWS), 1)
    first = (lane >> 4) * QUOTA
    want = ((lane & 15) + 1).astype(F32)
    hit = (inside >= first) & (inside < first + QUOTA) & (slot == want)
    return hit.astype(F32).astype(BF)


def head_mask():
    row, lane = iota((SHARE * WIDE, COLS), 0), iota((SHARE * WIDE, COLS), 1)
    low = jnp.where(row >= WIDE, HEAD, 0)
    return ((lane >= low) & (lane < low + HEAD)).astype(F32).astype(BF)


def first_head(member):
    return (member >> 1) + 4 * (member & 1)


def member_columns():
    row, col = iota((C, MEMBERS * LANE), 0), iota((C, MEMBERS * LANE), 1)
    lane = col & (LANE - 1)
    first = first_head(col >> 7) * HEAD + lane
    want = jnp.where(lane < HEAD, first, first + (MEMBERS - 1) * HEAD)
    want = jnp.where(lane < COLS, want, -1)
    return (row == want).astype(F32).astype(BF)


def allowed_pairs(member, seg_ref, dil_ref, cut):
    left, right = iota((WIDE, WIDE), 0), iota((WIDE, WIDE), 1)
    slot_left, slot_right = left & 15, right & 15
    run_left, run_right = slot_left >= cut, slot_right >= cut
    pos_left = jnp.where(run_left, slot_left - cut, slot_left)
    pos_right = jnp.where(run_right, slot_right - cut, slot_right)
    apart = pos_left ^ pos_right
    apart = jnp.where(run_left != run_right, apart | 256, apart)
    apart = jnp.where((left >> 4) != (right >> 4), apart | 256, apart)
    parts = []
    for h in range(SHARE):
        head = first_head(member) + MEMBERS * h
        seg, dil = seg_ref[head], dil_ref[head]
        parts.append(apart & (~(seg - 1) | (dil - 1)))
    return jnp.concatenate(parts, axis=0) == 0


def attention(block, upstream, w3_ref, mask, allowed):
    scale = HEAD ** (-0.5)
    weights = [w3_ref[part].reshape(COLS, C) for part in range(3)]
    query, key, value = [dot_last(block, each).astype(BF) for each in weights]
    many_query = jnp.concatenate([query] * SHARE, axis=0) * mask
    many_grad = jnp.concatenate([upstream] * SHARE, axis=0) * mask
    scores = dot_last(many_query, key) * scale
    masked = jnp.where(allowed, scores, -1e30)
    top = jnp.max(masked, axis=1, keepdims=True)
    expo = jnp.where(allowed, jnp.exp(masked - top), 0.0)
    prob = expo / jnp.sum(expo, axis=1, keepdims=True)
    prob_bf = prob.astype(BF)
    mask_f = mask.astype(F32)

    def own_head(full):
        return jnp.sum((full * mask_f).reshape(SHARE, WIDE, COLS), axis=0)

    mixed = own_head(dot(prob_bf, value))
    dprob = dot_last(many_grad, value)
    dscore = (prob * (dprob - jnp.sum(prob * dprob, axis=1, keepdims=True)) * scale).astype(BF)
    dquery = own_head(dot(dscore, key)).astype(BF)
    dkey = dot_first(dscore, many_query).astype(BF)
    dvalue = dot_first(prob_bf, many_grad).astype(BF)
    total = dot(dquery, weights[0]) + dot(dkey, weights[1]) + dot(dvalue, weights[2])
    return mixed, total


def shift(index, by, size):
    return (index + by + size) & (size - 1)


def place_of(member, y):
    return (member >> 1) * 8 + y * 2 + (member & 1)


class Weights:
    def __init__(self, w3_ref, own_ref, send_sems, recv_sems, share_sems):
        self.w3_ref, self.own_ref = w3_ref, own_ref
        self.send, self.recv, self.share = send_sems, recv_sems, share_sems
        self.tile, self.me = lax.axis_index("tile"), lax.axis_index("slide")
        self.y = (self.tile >> 1) & 3
        self.member = (self.tile >> 3) * 2 + (self.tile & 1)
        self.carrier = self.y < 3
        self.row = pl.multiple_of(jnp.minimum(self.y, 2) * 16, 16)
        self.first = first_head(self.member)

    def greet(self):
        @pl.when(self.carrier)
        def _():
            for head in range(SHARE):
                source = self.first + MEMBERS * head
                j = shift(self.me, -source, SLIDES)

                @pl.when(j != 0)
                def _():
                    pl.semaphore_signal(
                        pltpu.get_barrier_semaphore(), inc=1,
                        device_id={"tile": place_of(j & 7, self.y), "slide": source}, device_id_type=MESH)

    def greetings(self):
        return jnp.where(self.carrier, jnp.where(self.member == 0, 1, 2), 0)

    def along_z(self, k):
        low = self.me & 7
        target = ((low & 3) << 1) | (low >> 2)
        return pltpu.make_async_remote_copy(
            self.own_ref, self.w3_ref.at[:, self.me >> 3, pl.ds(self.row, 16)],
            self.send.at[k], self.recv.at[self.me >> 3],
            device_id={"tile": place_of(target, self.y), "slide": shift(self.me, self.member + 8 * k, SLIDES)},
            device_id_type=MESH)

    def along_y(self, j):
        peer = (self.tile & ~6) | (((self.y + j) & 3) << 1)
        rows = self.w3_ref.at[:, :, pl.ds(self.row, 16)]
        return pltpu.make_async_remote_copy(
            rows, rows, self.share.at[3 + j], self.share.at[jnp.minimum(self.y, 2)],
            device_id={"tile": peer}, device_id_type=MESH)

    def start(self, wq_ref):
        @pl.when(self.carrier)
        def _():
            for part in range(3):
                self.own_ref[part] = wq_ref[pl.ds(pl.multiple_of(part * HEAD + self.row, 16), 16)]

            self.along_z(1).start()

            @pl.when(self.member != 0)
            def _():
                self.along_z(0).start()

            @pl.when((self.me & 7) == self.first)
            def _():
                self.w3_ref[:, self.me >> 3, pl.ds(self.row, 16)] = self.own_ref[...]

    def hand_on(self):
        @pl.when(self.carrier)
        def _():
            for head in range(SHARE):

                @pl.when(self.me != self.first + MEMBERS * head)
                def _():
                    rows = self.w3_ref.at[:, head, pl.ds(0, 16)]
                    pltpu.make_async_copy(rows, rows, self.recv.at[head]).wait()

            for j in range(1, 4):
                self.along_y(j).start()

    def finish(self):
        for y in range(3):

            @pl.when(self.y != y)
            def _():
                rows = self.w3_ref.at[:, :, pl.ds(16 * y, 16)]
                pltpu.make_async_copy(rows, rows, self.share.at[y]).wait()

    def end(self):
        @pl.when(self.carrier)
        def _():
            self.along_z(1).wait_send()

            @pl.when(self.member != 0)
            def _():
                self.along_z(0).wait_send()

            for j in range(1, 4):
                self.along_y(j).wait_send()


def members_start(out_ref, in_ref, sems, n, same=False):
    tile = lax.axis_index("tile")
    member = (tile >> 3) * 2 + (tile & 1)
    if not same:
        in_ref[member] = out_ref[member]

    @pl.loop(1, MEMBERS)
    def _(j):
        peer = shift(member, j, MEMBERS)
        pltpu.make_async_remote_copy(
            in_ref.at[member] if same else out_ref.at[peer], in_ref.at[member],
            sems.at[0, n], sems.at[1, n],
            device_id={"tile": (peer >> 1) * 8 + (tile & 6) + (peer & 1)}, device_id_type=MESH).start()


def members_wait(in_ref, sems, n):
    some = in_ref.at[pl.ds(0, MEMBERS - 1)]
    pltpu.make_async_copy(some, some, sems.at[1, n]).wait()
    pltpu.make_async_copy(some, some, sems.at[0, n]).wait()


def exchange_start(out_ref, in_ref, send_sem, recv_sem):
    me = lax.axis_index("slide")
    in_ref[me] = out_ref[me]

    @pl.loop(1, SLIDES)
    def _(j):
        peer = shift(me, j, SLIDES)
        pltpu.make_async_remote_copy(
            out_ref.at[peer], in_ref.at[me], send_sem, recv_sem,
            device_id={"slide": peer}, device_id_type=MESH).start()


def exchange_wait(out_ref, in_ref, send_sem, recv_sem):
    some = pl.ds(0, SLIDES - 1)
    pltpu.make_async_copy(in_ref.at[some], in_ref.at[some], recv_sem).wait()
    pltpu.make_async_copy(out_ref.at[some], out_ref.at[some], send_sem).wait()


def greet():
    tile, me = lax.axis_index("tile"), lax.axis_index("slide")
    barrier = pltpu.get_barrier_semaphore()

    @pl.loop(1, SLIDES)
    def _(j):
        pl.semaphore_signal(
            barrier, inc=1, device_id={"slide": shift(me, j, SLIDES)}, device_id_type=MESH)

    @pl.loop(1, PLANE)
    def _(j):
        pl.semaphore_signal(
            barrier, inc=1, device_id={"tile": shift(tile, j, PLANE)}, device_id_type=MESH)


def greeted(more):
    pl.semaphore_wait(pltpu.get_barrier_semaphore(), SLIDES + PLANE - 2 + more)


def conv_grads(dpool, gain, cv_ref, inv_ref):
    grad = dpool * (gain * (1.0 / AREA))
    level = grad - jnp.mean(grad, axis=1, keepdims=True)

    def step(b, total):
        some = pl.ds(b * SIDE, SIDE)
        along = jnp.mean(cv_ref[some] * grad, axis=2, keepdims=True)
        dconv = inv_ref[some][:, :, :1] * (level - cv_ref[some] * along)
        cv_ref[some] = dconv
        return total + jnp.sum(dconv, axis=0)

    return lax.fori_loop(0, SIDE, step, jnp.zeros((ROWS, C), F32))


def tap_grads(chunk, xp_ref, yp_ref, cv_ref, sp_ref):
    lanes = pl.ds(pl.multiple_of(chunk * LANE, LANE), LANE)
    for i in range(SIDE):
        row = [cv_ref[i * SIDE + j, :, lanes] for j in range(SIDE)]
        for f, point in enumerate(points(row[::-1])):
            yp_ref[f, i] = point

    @pl.loop(0, POINTS, unroll=5)
    def _(f):
        cells = [xp_ref[f, i, :, lanes] for i in range(SIDE)]
        grads = [yp_ref[f, i] for i in range(SIDE)]
        for r in range(TAPS):
            total = None
            for i in range(*row_span(r - REACH)):
                term = cells[i + r - REACH] * grads[i]
                total = term if total is None else total + term
            sp_ref[f, r : r + 1] = jnp.sum(total, axis=0, keepdims=True)

    return coefficients([sp_ref[f] * POINT_SCALE[f] for f in range(POINTS)])[1:]


def unit_at(ref, unit):
    rows = pl.ds(pl.multiple_of((unit & 3) * 16, 16), 16)
    lanes = pl.ds(pl.multiple_of((unit >> 2) * LANE, LANE), LANE)
    return ref.at[rows, lanes]


def owner_of(unit):
    return unit + ((unit * 11) >> 5)


def send_chunk(chunk, flat_ref, near_ref, sems):
    tile = lax.axis_index("tile")
    for rows in range(4):
        unit = chunk * 4 + rows
        peer = owner_of(unit)

        @pl.when(peer != tile)
        def _():
            pltpu.make_async_remote_copy(
                unit_at(flat_ref, unit), near_ref.at[tile], sems.at[0], sems.at[1],
                device_id={"tile": peer}, device_id_type=MESH).start()


def reduce_all(flat_ref, near_ref, far_ref, res_ref, far_out_ref, sems):
    tile, me = lax.axis_index("tile"), lax.axis_index("slide")
    owner = (tile & 3) != 3
    unit = jnp.minimum((tile >> 2) * 3 + (tile & 3), UNITS - 1)

    def wait_units(ref, count, sem):
        some = pl.ds(0, count)
        pltpu.make_async_copy(ref.at[some], ref.at[some], sem).wait()

    @pl.when(owner)
    def _():
        near_ref[tile] = unit_at(flat_ref, unit)[...]
        wait_units(near_ref, PLANE - 1, sems.at[1])
        wait_units(near_ref, UNITS - 1, sems.at[0])
        near = jnp.sum(near_ref[...].astype(F32), axis=0).astype(BF)
        far_out_ref[0] = near
        far_ref[me] = near

        @pl.loop(1, SLIDES)
        def _(j):
            pltpu.make_async_remote_copy(
                far_out_ref.at[0], far_ref.at[me], sems.at[2], sems.at[3],
                device_id={"slide": shift(me, j, SLIDES)}, device_id_type=MESH).start()

        wait_units(far_ref, SLIDES - 1, sems.at[3])
        far_out_ref[1] = jnp.sum(far_ref[...].astype(F32), axis=0).astype(BF)
        pltpu.make_async_copy(far_out_ref.at[1], unit_at(res_ref, unit), sems.at[5]).start()

        @pl.loop(1, PLANE)
        def _(j):
            pltpu.make_async_remote_copy(
                far_out_ref.at[1], unit_at(res_ref, unit), sems.at[4], sems.at[5],
                device_id={"tile": shift(tile, j, PLANE)}, device_id_type=MESH).start()

        wait_units(far_ref, SLIDES - 1, sems.at[2])
        wait_units(near_ref, PLANE - 1, sems.at[4])

    @pl.when(jnp.logical_not(owner))
    def _():
        wait_units(near_ref, UNITS, sems.at[0])

    pltpu.make_async_copy(res_ref, res_ref, sems.at[5]).wait()


def step_kernel(
    maps_ref, dw_ref, bias_ref, gain_ref, win_hbm, wq_ref, seg_ref, dil_ref, slot_ref, len_ref, cot_ref,
    attn_ref, sums_ref,
    rows_ref, xt_ref, cv_ref, inv_ref, wb_ref, win_ref, w3_ref, own_ref,
    out_ref, in_ref, back_out_ref, back_in_ref,
    pick_ref, cot_out_ref, cot_in_ref, blocks_ref, part_out_ref, part_in_ref, mixed_out_ref, mixed_in_ref,
    xp_ref, yp_ref, sp_ref, norm_ref, flat_ref, near_ref, far_ref, far_out_ref, res_ref,
    local_sems, weight_send, weight_recv, share_sems, member_sems, route_sems, sum_sems,
):
    greet()
    weights = Weights(w3_ref, own_ref, weight_send, weight_recv, share_sems)
    weights.greet()
    for r in range(SIDE):
        map_copy(maps_ref, rows_ref, local_sems, r).start()
    win_copy = pltpu.make_async_copy(win_hbm, win_ref, local_sems.at[SIDE])
    win_copy.start()
    member = weights.member
    pick_ref[...] = member_columns()
    cots = dot(cot_ref[...], pick_ref[...])
    cut = jnp.full((ROWS, LANE), len_ref[0, 0], jnp.int32).astype(F32)
    spare = iota((ROWS, LANE), 1) >= COLS
    for m in range(MEMBERS):
        cot_out_ref[m] = jnp.where(spare, cut, cots[:, m * LANE : (m + 1) * LANE]).astype(BF)
    spread_taps(dw_ref, wb_ref)
    transpose_maps(maps_ref, rows_ref, local_sems, xt_ref)
    greeted(weights.greetings())
    weights.start(wq_ref)
    members_start(cot_out_ref, cot_in_ref, member_sems, 0)

    @pl.loop(0, CHUNKS)
    def _(chunk):
        conv_chunk(chunk, xt_ref, xp_ref, yp_ref, wb_ref, bias_ref, cv_ref)

    total = normalise(cv_ref, inv_ref, (0, SIDE), jnp.zeros((ROWS, C), F32))
    gain = gain_ref[...].reshape(1, C)
    pooled = (total * gain * (1.0 / AREA)).astype(BF)
    win_copy.wait()
    embed = dot(pooled, win_ref[...]).astype(BF)

    select, slots = send_rows(slot_ref)
    packed = jnp.concatenate([spread(embed), slots], axis=0)
    out_ref[...] = dot(select, packed).astype(BF).reshape(SLIDES, PACK, LANE)
    exchange_start(out_ref, in_ref, route_sems.at[0], route_sems.at[1])
    weights.hand_on()
    spread_slots, mask = slot_spread(), head_mask()
    members_wait(cot_in_ref, member_sems, 0)
    upstream = cot_in_ref[...].reshape(WIDE, LANE)
    cut = upstream[:, COLS : COLS + 1].astype(F32).astype(jnp.int32)
    allowed = allowed_pairs(member, seg_ref, dil_ref, cut)
    exchange_wait(out_ref, in_ref, route_sems.at[0], route_sems.at[1])
    arrived = in_ref[...].reshape(SLIDES * PACK, LANE)
    place = place_rows(spread_slots, arrived)
    blocks_ref[member] = gather_chunks(dot_first(place, arrived).astype(BF))
    members_start(None, blocks_ref, member_sems, 1, True)
    weights.finish()
    members_wait(blocks_ref, member_sems, 1)
    mixed, partial = attention(
        blocks_ref[...].reshape(WIDE, C), upstream[:, :COLS], w3_ref, mask, allowed)
    part_out_ref[...] = partial.astype(BF).reshape(MEMBERS, ROWS, C)
    members_start(part_out_ref, part_in_ref, member_sems, 2)
    padded = jnp.concatenate([mixed, jnp.zeros((WIDE, LANE - COLS), F32)], axis=1)
    mixed_out_ref[...] = padded.astype(BF).reshape(MEMBERS, ROWS, LANE)
    members_start(mixed_out_ref, mixed_in_ref, member_sems, 3)
    members_wait(part_in_ref, member_sems, 2)
    dblock = jnp.sum(part_in_ref[...].astype(F32), axis=0).astype(BF)
    back_out_ref[...] = dot(place, spread(dblock)).astype(BF).reshape(SLIDES, PACK, LANE)
    exchange_start(back_out_ref, back_in_ref, route_sems.at[2], route_sems.at[3])
    members_wait(mixed_in_ref, member_sems, 3)
    every = jnp.concatenate([mixed_in_ref[m] for m in range(MEMBERS)], axis=1)
    attn_ref[...] = dot_last(every, pick_ref[...]).astype(BF)
    weights.end()
    exchange_wait(back_out_ref, back_in_ref, route_sems.at[2], route_sems.at[3])
    returned = back_in_ref[...].reshape(SLIDES * PACK, LANE)
    dembed = gather_chunks(dot_first(select[:, : CHUNKS * ROWS], returned).astype(BF))
    dpool = dot_last(dembed, win_ref[...])

    bias_grad = conv_grads(dpool, gain, cv_ref, inv_ref)
    norm_ref[0:1] = jnp.sum(bias_grad, axis=0, keepdims=True)
    norm_ref[1:2] = jnp.sum(dpool * total, axis=0, keepdims=True) * (1.0 / AREA)
    sp_ref[...] = jnp.zeros(sp_ref.shape, F32)

    @pl.loop(0, CHUNKS)
    def _(chunk):
        lanes = pl.ds(pl.multiple_of(chunk * LANE, LANE), LANE)
        blocks = tap_grads(chunk, xp_ref, yp_ref, cv_ref, sp_ref)
        last = iota((8, LANE), 0) == TAPS
        for k in range(2):
            blocks[k] = jnp.where(last, norm_ref[k : k + 1, lanes], blocks[k])
        blocks.append(jnp.zeros((8, LANE), F32))
        flat_ref[:, lanes] = jnp.concatenate(blocks, axis=0).astype(BF)
        send_chunk(chunk, flat_ref, near_ref, sum_sems)

    reduce_all(flat_ref, near_ref, far_ref, res_ref, far_out_ref, sum_sems)
    sums_ref[...] = res_ref[...]


def finish_kernel(attn_ref, res_ref, out_ref, kernel_ref, norm_ref):
    out_ref[...] = attn_ref[...]
    result = res_ref[...].astype(F32)
    for r in range(TAPS):
        for s in range(TAPS):
            kernel_ref[r * TAPS + s : r * TAPS + s + 1] = result[s * 8 + r : s * 8 + r + 1]
    for k in range(2):
        norm_ref[k : k + 1] = result[k * 8 + TAPS : k * 8 + TAPS + 1]


VMEM_LIMIT = 60 * 1024 * 1024


def params(**extra):
    return pltpu.CompilerParams(vmem_limit_bytes=VMEM_LIMIT, **extra)


def vmem(count):
    return [pl.BlockSpec(memory_space=pltpu.VMEM)] * count


def smem(count):
    return [pl.BlockSpec(memory_space=pltpu.SMEM)] * count


def shape(*dims, kind=BF):
    return jax.ShapeDtypeStruct(dims, kind)


def body(
    tile_maps, dw_kernel, conv_bias, norm_gain, w_in, w_qkv, seg_len, dilation,
    tile_slot, slide_lengths, cotangent,
):
    dma = pltpu.SemaphoreType.DMA
    hbm = [pl.BlockSpec(memory_space=pl.ANY)]
    message = pltpu.VMEM((SLIDES, PACK, LANE), BF)
    wide = pltpu.VMEM((MEMBERS, ROWS, C), BF)
    narrow = pltpu.VMEM((MEMBERS, ROWS, LANE), BF)
    attn, sums = pl.pallas_call(
        step_kernel,
        out_shape=[shape(ROWS, C), shape(SUM_ROWS, C)],
        in_specs=hbm + vmem(3) + hbm + vmem(1) + smem(4) + vmem(1),
        out_specs=vmem(2),
        scratch_shapes=[
            pltpu.VMEM((SIDE, ROWS, SIDE, C), BF), pltpu.VMEM((SIDE, SIDE, ROWS, C), F32),
            pltpu.VMEM((AREA, ROWS, C), F32), pltpu.VMEM((AREA, ROWS, LANE), F32),
            pltpu.VMEM((POINTS, TAPS, 8, C), F32), pltpu.VMEM((C, C), BF),
            pltpu.VMEM((3, SHARE, HEAD, C), BF), pltpu.VMEM((3, 16, C), BF), message, message, message, message,
            pltpu.VMEM((C, MEMBERS * LANE), BF), narrow, narrow, wide, wide, wide, narrow, narrow,
            pltpu.VMEM((POINTS, SIDE, ROWS, C), F32), pltpu.VMEM((POINTS, SIDE, ROWS, LANE), F32),
            pltpu.VMEM((POINTS, 8, LANE), F32), pltpu.VMEM((2, C), F32), pltpu.VMEM((SUM_ROWS, C), BF),
            pltpu.VMEM((PLANE, 16, LANE), BF), pltpu.VMEM((SLIDES, 16, LANE), BF),
            pltpu.VMEM((2, 16, LANE), BF), pltpu.VMEM((SUM_ROWS, C), BF),
            dma((9,)), dma((2,)), dma((2,)), dma((7,)), dma((2, 4)), dma((4,)), dma((6,)),
        ],
        compiler_params=params(collective_id=1, has_side_effects=True),
    )(
        tile_maps, dw_kernel, conv_bias, norm_gain, w_in, w_qkv.T,
        seg_len, dilation, tile_slot, slide_lengths, cotangent,
    )
    return pl.pallas_call(
        finish_kernel,
        out_shape=[shape(ROWS, C), shape(49, C, kind=F32), shape(2, C, kind=F32)],
        in_specs=vmem(2),
        out_specs=vmem(3),
    )(attn, sums)


def solution(mesh):
    both = ("tile", "slide")
    in_specs = (
        P(both, None, None, None), P(), P(), P(), P(), P(None, "slide"), P(), P(),
        P(both), P(both, None), P(both, None),
    )
    out_specs = (P(both, None), P(), P())
    return jax.shard_map(body, mesh=mesh, in_specs=in_specs, out_specs=out_specs, check_vma=False)
```

```python
import jax
import jax.numpy as jnp
from jax import lax
from jax.experimental import pallas as pl
from jax.experimental.pallas import tpu as pltpu
from jax.sharding import PartitionSpec as P

NORM_EPS = 1e-06
MESH = pl.DeviceIdType.MESH
BF = jnp.bfloat16
F32 = jnp.float32

SIDE = 8
AREA = SIDE * SIDE
REACH = 3
TAPS = 7
ROWS = 16
C = 768
LANE = 128
CHUNKS = C // LANE
HEADS = 16
HEAD = 48
SLIDES = 16
PLANE = 32
QUOTA = 3
PACK = 32
MEMBERS = 8
SHARE = HEADS // MEMBERS
WIDE = MEMBERS * ROWS
COLS = SHARE * HEAD
UNITS = 24
SUM_ROWS = 64


def iota(shape, dim):
    return lax.broadcasted_iota(jnp.int32, shape, dim)


def dot(left, right):
    return jnp.dot(left, right, preferred_element_type=F32)


def dot_last(left, right):
    return lax.dot_general(left, right, (((1,), (1,)), ((), ())), preferred_element_type=F32)


def dot_first(left, right):
    return lax.dot_general(left, right, (((0,), (0,)), ((), ())), preferred_element_type=F32)


def spread(block):
    return jnp.concatenate([block[:, k * LANE : (k + 1) * LANE] for k in range(CHUNKS)], axis=0)


def gather_chunks(stack):
    return jnp.concatenate([stack[k * ROWS : (k + 1) * ROWS] for k in range(CHUNKS)], axis=1)


def row_span(offset):
    return max(0, -offset), min(SIDE, SIDE - offset)


def map_copy(maps_ref, rows_ref, sems, r):
    return pltpu.make_async_copy(maps_ref.at[:, r], rows_ref.at[r], sems.at[r])


def transpose_maps(maps_ref, rows_ref, sems, xt_ref):
    row, col = iota((128, 128), 0), iota((128, 128), 1)
    perm = ((row >> 4) == (col & 7)) & ((row & 15) == (col >> 3))
    perm = perm.astype(F32).astype(BF)
    for r in range(SIDE):
        map_copy(maps_ref, rows_ref, sems, r).wait()
        part = rows_ref[r].astype(F32).reshape(128, C).astype(BF)
        xt_ref[r] = dot(perm, part).reshape(SIDE, ROWS, C)


POINTS = 20


def points(a):
    u = [a[0] + a[6], a[1] + a[7] if len(a) > 7 else a[1]] + a[2:6]
    v = [a[0] - a[6], a[1] - a[7] if len(a) > 7 else a[1]] + a[2:6]
    p = [u[k] + u[k + 3] for k in range(3)]
    q = [u[k] - u[k + 3] for k in range(3)]
    c0, c1 = p[0] - p[2], p[1] - p[2]
    e0, e1 = q[0] - q[2], q[1] + q[2]
    g0, g1 = v[0] - v[2] + v[4], v[1] - v[3] + v[5]
    h0, h1, h2, h3 = v[0] - v[4], v[1] - v[5], v[2] + v[4], v[3] + v[5]
    s0, s1 = h0 + h2, h1 + h3
    return [
        p[0] + p[1] + p[2], c0, c1, c0 + c1, q[0] - q[1] + q[2], e0, e1, e0 + e1,
        g0, g1, g0 + g1, h0, h1, h0 + h1, h2, h3, h2 + h3, s0, s1, s0 + s1,
    ]


POINT_SCALE = [0.25] * 8 + [0.5] * 12


def coefficients(m):
    third = 1.0 / 3.0
    c0, c1 = m[1] - m[2], m[3] - m[1] - m[2] - m[2]
    p2 = (m[0] - c0 - c1) * third
    p = [c0 + p2, c1 + p2, p2]
    e0, e1 = m[5] - m[6], m[7] - m[5]
    q2 = (m[4] - e0 + e1) * third
    q = [e0 + q2, e1 - q2, q2]
    u = [p[k] + q[k] for k in range(3)] + [p[k] - q[k] for k in range(3)]
    g0, g1 = m[8] - m[9], m[10] - m[8] - m[9]
    a1, b1, s1 = m[13] - m[11] - m[12], m[16] - m[14] - m[15], m[19] - m[17] - m[18]
    s0, s2 = m[17] - m[11], m[18] - m[12]
    h0 = m[11] - m[14] - s2
    h1 = a1 - b1
    h2 = m[12] - m[15] + s0 + s2
    h3 = s1 - a1
    v4, v5 = (g0 - h0 + h2) * third, (g1 - h1 + h3) * third
    v = [h0 + v4, h1 + v5, h2 - v4, h3 - v5, v4, v5]
    return [u[k] + v[k] for k in (3, 4, 5)] + [u[k] - v[k] for k in range(5)]


def spread_taps(dw_ref, wb_ref):
    taps = dw_ref[...].astype(F32)
    for r in range(TAPS):
        row = [taps[r * TAPS + s : r * TAPS + s + 1] for s in range(TAPS)]
        for f, point in enumerate(points(row[::-1])):
            wb_ref[f, r] = jnp.broadcast_to(point * POINT_SCALE[f], (8, C))


def conv_chunk(chunk, xt_ref, xp_ref, yp_ref, wb_ref, bias_ref, cv_ref):
    lanes = pl.ds(pl.multiple_of(chunk * LANE, LANE), LANE)
    bias = jnp.broadcast_to(bias_ref[lanes].reshape(1, LANE), (ROWS, LANE))
    for i in range(SIDE):
        for f, point in enumerate(points([xt_ref[i, j, :, lanes] for j in range(SIDE)])):
            xp_ref[f, i, :, lanes] = point

    @pl.loop(0, POINTS, unroll=10)
    def _(f):
        cells = [xp_ref[f, i, :, lanes].reshape(2, 8, LANE) for i in range(SIDE)]
        taps = [wb_ref[f, r, :, lanes] for r in range(TAPS)]
        for i in range(SIDE):
            total = None
            for r in range(TAPS):
                if 0 <= i + r - REACH < SIDE:
                    term = cells[i + r - REACH] * taps[r]
                    total = term if total is None else total + term
            yp_ref[f, i] = total.reshape(ROWS, LANE)

    for i in range(SIDE):
        for j, value in enumerate(coefficients([yp_ref[f, i] for f in range(POINTS)])):
            cv_ref[i * SIDE + j, :, lanes] = value + bias


def normalise(cv_ref, inv_ref, rows, total):
    def step(b, total):
        some = pl.ds(b * SIDE, SIDE)
        mean = jnp.mean(cv_ref[some], axis=2, keepdims=True)
        centered = cv_ref[some] - mean
        inv = lax.rsqrt(jnp.mean(centered * centered, axis=2, keepdims=True) + NORM_EPS)
        normed = (cv_ref[some] - mean) * inv
        cv_ref[some] = normed
        inv_ref[some] = jnp.broadcast_to(inv, (SIDE, ROWS, LANE))
        return total + jnp.sum(normed, axis=0)

    return lax.fori_loop(rows[0], rows[1], step, total)


def send_rows(slot_ref):
    lane = iota((1, 112), 1)
    tile, chunk = lane & 15, lane >> 4
    owner = jnp.zeros((1, 112), jnp.int32)
    for t in range(ROWS):
        owner = jnp.where(tile == t, slot_ref[t] >> 4, owner)
    rank = jnp.zeros((1, 112), jnp.int32)
    for t in range(ROWS):
        rank = rank + jnp.where((owner == (slot_ref[t] >> 4)) & (tile > t), 1, 0)
    want = owner * PACK + chunk * QUOTA + rank
    select = (iota((SLIDES * PACK, 112), 0) == want).astype(F32).astype(BF)
    sub = iota((ROWS, LANE), 0)
    slots = jnp.zeros((ROWS, LANE), jnp.int32)
    for t in range(ROWS):
        slots = jnp.where(sub == t, (slot_ref[t] & 15) + 1, slots)
    return select, slots.astype(F32).astype(BF)


def slot_spread():
    size = SLIDES * PACK
    row, col = iota((size, size), 0), iota((size, size), 1)
    inside = row & (PACK - 1)
    quota = inside
    for k in range(1, PACK // QUOTA + 1):
        quota = jnp.where(inside >= k * QUOTA, inside - k * QUOTA, quota)
    return (col == (row - inside + CHUNKS * QUOTA + quota)).astype(F32).astype(BF)


def place_rows(spread_slots, arrived):
    size = SLIDES * PACK
    slot = dot(spread_slots, arrived)[:, : CHUNKS * ROWS]
    inside = iota((size, CHUNKS * ROWS), 0) & (PACK - 1)
    lane = iota((size, CHUNKS * ROWS), 1)
    first = (lane >> 4) * QUOTA
    want = ((lane & 15) + 1).astype(F32)
    hit = (inside >= first) & (inside < first + QUOTA) & (slot == want)
    return hit.astype(F32).astype(BF)


def head_mask():
    row, lane = iota((SHARE * WIDE, COLS), 0), iota((SHARE * WIDE, COLS), 1)
    low = jnp.where(row >= WIDE, HEAD, 0)
    return ((lane >= low) & (lane < low + HEAD)).astype(F32).astype(BF)


def first_head(member):
    return (member >> 1) + 4 * (member & 1)


def member_columns():
    row, col = iota((C, MEMBERS * LANE), 0), iota((C, MEMBERS * LANE), 1)
    lane = col & (LANE - 1)
    first = first_head(col >> 7) * HEAD + lane
    want = jnp.where(lane < HEAD, first, first + (MEMBERS - 1) * HEAD)
    want = jnp.where(lane < COLS, want, -1)
    return (row == want).astype(F32).astype(BF)


def allowed_pairs(member, seg_ref, dil_ref, cut):
    left, right = iota((WIDE, WIDE), 0), iota((WIDE, WIDE), 1)
    slot_left, slot_right = left & 15, right & 15
    run_left, run_right = slot_left >= cut, slot_right >= cut
    pos_left = jnp.where(run_left, slot_left - cut, slot_left)
    pos_right = jnp.where(run_right, slot_right - cut, slot_right)
    apart = pos_left ^ pos_right
    apart = jnp.where(run_left != run_right, apart | 256, apart)
    apart = jnp.where((left >> 4) != (right >> 4), apart | 256, apart)
    parts = []
    for h in range(SHARE):
        head = first_head(member) + MEMBERS * h
        seg, dil = seg_ref[head], dil_ref[head]
        parts.append(apart & (~(seg - 1) | (dil - 1)))
    return jnp.concatenate(parts, axis=0) == 0


def attention(block, upstream, w3_ref, mask, allowed):
    scale = HEAD ** (-0.5)
    weights = [w3_ref[part].reshape(COLS, C) for part in range(3)]
    query, key, value = [dot_last(block, each).astype(BF) for each in weights]
    many_query = jnp.concatenate([query] * SHARE, axis=0) * mask
    many_grad = jnp.concatenate([upstream] * SHARE, axis=0) * mask
    scores = dot_last(many_query, key) * scale
    masked = jnp.where(allowed, scores, -1e30)
    top = jnp.max(masked, axis=1, keepdims=True)
    expo = jnp.where(allowed, jnp.exp(masked - top), 0.0)
    prob = expo / jnp.sum(expo, axis=1, keepdims=True)
    prob_bf = prob.astype(BF)
    mask_f = mask.astype(F32)

    def own_head(full):
        return jnp.sum((full * mask_f).reshape(SHARE, WIDE, COLS), axis=0)

    mixed = own_head(dot(prob_bf, value))
    dprob = dot_last(many_grad, value)
    dscore = (prob * (dprob - jnp.sum(prob * dprob, axis=1, keepdims=True)) * scale).astype(BF)
    dquery = own_head(dot(dscore, key)).astype(BF)
    dkey = dot_first(dscore, many_query).astype(BF)
    dvalue = dot_first(prob_bf, many_grad).astype(BF)
    total = dot(dquery, weights[0]) + dot(dkey, weights[1]) + dot(dvalue, weights[2])
    return mixed, total


def shift(index, by, size):
    return (index + by + size) & (size - 1)


def place_of(member, y):
    return (member >> 1) * 8 + y * 2 + (member & 1)


class Weights:
    def __init__(self, w3_ref, own_ref, send_sems, recv_sems, share_sems):
        self.w3_ref, self.own_ref = w3_ref, own_ref
        self.send, self.recv, self.share = send_sems, recv_sems, share_sems
        self.tile, self.me = lax.axis_index("tile"), lax.axis_index("slide")
        self.y = (self.tile >> 1) & 3
        self.member = (self.tile >> 3) * 2 + (self.tile & 1)
        self.carrier = self.y < 3
        self.row = pl.multiple_of(jnp.minimum(self.y, 2) * 16, 16)
        self.first = first_head(self.member)

    def greet(self):
        @pl.when(self.carrier)
        def _():
            for head in range(SHARE):
                source = self.first + MEMBERS * head
                j = shift(self.me, -source, SLIDES)

                @pl.when(j != 0)
                def _():
                    pl.semaphore_signal(
                        pltpu.get_barrier_semaphore(), inc=1,
                        device_id={"tile": place_of(j & 7, self.y), "slide": source}, device_id_type=MESH)

    def greetings(self):
        return jnp.where(self.carrier, jnp.where(self.member == 0, 1, 2), 0)

    def along_z(self, k):
        low = self.me & 7
        target = ((low & 3) << 1) | (low >> 2)
        return pltpu.make_async_remote_copy(
            self.own_ref, self.w3_ref.at[:, self.me >> 3, pl.ds(self.row, 16)],
            self.send.at[k], self.recv.at[self.me >> 3],
            device_id={"tile": place_of(target, self.y), "slide": shift(self.me, self.member + 8 * k, SLIDES)},
            device_id_type=MESH)

    def along_y(self, j):
        peer = (self.tile & ~6) | (((self.y + j) & 3) << 1)
        rows = self.w3_ref.at[:, :, pl.ds(self.row, 16)]
        return pltpu.make_async_remote_copy(
            rows, rows, self.share.at[3 + j], self.share.at[jnp.minimum(self.y, 2)],
            device_id={"tile": peer}, device_id_type=MESH)

    def start(self, wq_ref):
        @pl.when(self.carrier)
        def _():
            for part in range(3):
                self.own_ref[part] = wq_ref[pl.ds(pl.multiple_of(part * HEAD + self.row, 16), 16)]

            self.along_z(1).start()

            @pl.when(self.member != 0)
            def _():
                self.along_z(0).start()

            @pl.when((self.me & 7) == self.first)
            def _():
                self.w3_ref[:, self.me >> 3, pl.ds(self.row, 16)] = self.own_ref[...]

    def hand_on(self):
        @pl.when(self.carrier)
        def _():
            for head in range(SHARE):

                @pl.when(self.me != self.first + MEMBERS * head)
                def _():
                    rows = self.w3_ref.at[:, head, pl.ds(0, 16)]
                    pltpu.make_async_copy(rows, rows, self.recv.at[head]).wait()

            for j in range(1, 4):
                self.along_y(j).start()

    def finish(self):
        for y in range(3):

            @pl.when(self.y != y)
            def _():
                rows = self.w3_ref.at[:, :, pl.ds(16 * y, 16)]
                pltpu.make_async_copy(rows, rows, self.share.at[y]).wait()

    def end(self):
        @pl.when(self.carrier)
        def _():
            self.along_z(1).wait_send()

            @pl.when(self.member != 0)
            def _():
                self.along_z(0).wait_send()

            for j in range(1, 4):
                self.along_y(j).wait_send()


def members_start(out_ref, in_ref, sems, n, same=False):
    tile = lax.axis_index("tile")
    member = (tile >> 3) * 2 + (tile & 1)
    if not same:
        in_ref[member] = out_ref[member]

    @pl.loop(1, MEMBERS)
    def _(j):
        peer = shift(member, j, MEMBERS)
        pltpu.make_async_remote_copy(
            in_ref.at[member] if same else out_ref.at[peer], in_ref.at[member],
            sems.at[0, n], sems.at[1, n],
            device_id={"tile": (peer >> 1) * 8 + (tile & 6) + (peer & 1)}, device_id_type=MESH).start()


def members_wait(in_ref, sems, n):
    some = in_ref.at[pl.ds(0, MEMBERS - 1)]
    pltpu.make_async_copy(some, some, sems.at[1, n]).wait()
    pltpu.make_async_copy(some, some, sems.at[0, n]).wait()


def exchange_start(out_ref, in_ref, send_sem, recv_sem):
    me = lax.axis_index("slide")
    in_ref[me] = out_ref[me]

    @pl.loop(1, SLIDES)
    def _(j):
        peer = shift(me, j, SLIDES)
        pltpu.make_async_remote_copy(
            out_ref.at[peer], in_ref.at[me], send_sem, recv_sem,
            device_id={"slide": peer}, device_id_type=MESH).start()


def exchange_wait(out_ref, in_ref, send_sem, recv_sem):
    some = pl.ds(0, SLIDES - 1)
    pltpu.make_async_copy(in_ref.at[some], in_ref.at[some], recv_sem).wait()
    pltpu.make_async_copy(out_ref.at[some], out_ref.at[some], send_sem).wait()


def greet():
    tile, me = lax.axis_index("tile"), lax.axis_index("slide")
    barrier = pltpu.get_barrier_semaphore()

    @pl.loop(1, SLIDES)
    def _(j):
        pl.semaphore_signal(
            barrier, inc=1, device_id={"slide": shift(me, j, SLIDES)}, device_id_type=MESH)

    @pl.loop(1, PLANE)
    def _(j):
        pl.semaphore_signal(
            barrier, inc=1, device_id={"tile": shift(tile, j, PLANE)}, device_id_type=MESH)


def greeted(more):
    pl.semaphore_wait(pltpu.get_barrier_semaphore(), SLIDES + PLANE - 2 + more)


def conv_grads(dpool, gain, cv_ref, inv_ref):
    grad = dpool * (gain * (1.0 / AREA))
    level = grad - jnp.mean(grad, axis=1, keepdims=True)

    def step(b, total):
        some = pl.ds(b * SIDE, SIDE)
        along = jnp.mean(cv_ref[some] * grad, axis=2, keepdims=True)
        dconv = inv_ref[some][:, :, :1] * (level - cv_ref[some] * along)
        cv_ref[some] = dconv
        return total + jnp.sum(dconv, axis=0)

    return lax.fori_loop(0, SIDE, step, jnp.zeros((ROWS, C), F32))


def tap_grads(chunk, xp_ref, yp_ref, cv_ref, sp_ref):
    lanes = pl.ds(pl.multiple_of(chunk * LANE, LANE), LANE)
    for i in range(SIDE):
        row = [cv_ref[i * SIDE + j, :, lanes] for j in range(SIDE)]
        for f, point in enumerate(points(row[::-1])):
            yp_ref[f, i] = point

    @pl.loop(0, POINTS, unroll=10)
    def _(f):
        cells = [xp_ref[f, i, :, lanes] for i in range(SIDE)]
        grads = [yp_ref[f, i] for i in range(SIDE)]
        for r in range(TAPS):
            total = None
            for i in range(*row_span(r - REACH)):
                term = cells[i + r - REACH] * grads[i]
                total = term if total is None else total + term
            sp_ref[f, r : r + 1] = jnp.sum(total, axis=0, keepdims=True)

    return coefficients([sp_ref[f] * POINT_SCALE[f] for f in range(POINTS)])[1:]


def unit_at(ref, unit):
    rows = pl.ds(pl.multiple_of((unit & 3) * 16, 16), 16)
    lanes = pl.ds(pl.multiple_of((unit >> 2) * LANE, LANE), LANE)
    return ref.at[rows, lanes]


def owner_of(unit):
    return unit + ((unit * 11) >> 5)


def send_chunk(chunk, flat_ref, near_ref, sems):
    tile = lax.axis_index("tile")
    for rows in range(4):
        unit = chunk * 4 + rows
        peer = owner_of(unit)

        @pl.when(peer != tile)
        def _():
            pltpu.make_async_remote_copy(
                unit_at(flat_ref, unit), near_ref.at[tile], sems.at[0], sems.at[1],
                device_id={"tile": peer}, device_id_type=MESH).start()


def reduce_all(flat_ref, near_ref, far_ref, res_ref, far_out_ref, sems):
    tile, me = lax.axis_index("tile"), lax.axis_index("slide")
    owner = (tile & 3) != 3
    unit = jnp.minimum((tile >> 2) * 3 + (tile & 3), UNITS - 1)

    def wait_units(ref, count, sem):
        some = pl.ds(0, count)
        pltpu.make_async_copy(ref.at[some], ref.at[some], sem).wait()

    @pl.when(owner)
    def _():
        near_ref[tile] = unit_at(flat_ref, unit)[...]
        wait_units(near_ref, PLANE - 1, sems.at[1])
        near = jnp.sum(near_ref[...].astype(F32), axis=0).astype(BF)
        far_out_ref[0] = near
        far_ref[me] = near

        @pl.loop(1, SLIDES)
        def _(j):
            pltpu.make_async_remote_copy(
                far_out_ref.at[0], far_ref.at[me], sems.at[2], sems.at[3],
                device_id={"slide": shift(me, j, SLIDES)}, device_id_type=MESH).start()

        wait_units(far_ref, SLIDES - 1, sems.at[3])
        far_out_ref[1] = jnp.sum(far_ref[...].astype(F32), axis=0).astype(BF)
        pltpu.make_async_copy(far_out_ref.at[1], unit_at(res_ref, unit), sems.at[5]).start()

        @pl.loop(1, PLANE)
        def _(j):
            pltpu.make_async_remote_copy(
                far_out_ref.at[1], unit_at(res_ref, unit), sems.at[4], sems.at[5],
                device_id={"tile": shift(tile, j, PLANE)}, device_id_type=MESH).start()

        wait_units(near_ref, UNITS - 1, sems.at[0])
        wait_units(far_ref, SLIDES - 1, sems.at[2])
        wait_units(near_ref, PLANE - 1, sems.at[4])

    @pl.when(jnp.logical_not(owner))
    def _():
        wait_units(near_ref, UNITS, sems.at[0])

    pltpu.make_async_copy(res_ref, res_ref, sems.at[5]).wait()


def step_kernel(
    maps_ref, dw_ref, bias_ref, gain_ref, win_hbm, wq_ref, seg_ref, dil_ref, slot_ref, len_ref, cot_ref,
    attn_ref, sums_ref,
    rows_ref, xt_ref, cv_ref, inv_ref, wb_ref, win_ref, w3_ref, own_ref,
    out_ref, in_ref, back_out_ref, back_in_ref,
    pick_ref, cot_out_ref, cot_in_ref, blocks_ref, part_out_ref, part_in_ref, mixed_out_ref, mixed_in_ref,
    xp_ref, yp_ref, sp_ref, norm_ref, flat_ref, near_ref, far_ref, far_out_ref, res_ref,
    local_sems, weight_send, weight_recv, share_sems, member_sems, route_sems, sum_sems,
):
    greet()
    weights = Weights(w3_ref, own_ref, weight_send, weight_recv, share_sems)
    weights.greet()
    for r in range(SIDE):
        map_copy(maps_ref, rows_ref, local_sems, r).start()
    win_copy = pltpu.make_async_copy(win_hbm, win_ref, local_sems.at[SIDE])
    win_copy.start()
    member = weights.member
    pick_ref[...] = member_columns()
    cots = dot(cot_ref[...], pick_ref[...])
    cut = jnp.full((ROWS, LANE), len_ref[0, 0], jnp.int32).astype(F32)
    spare = iota((ROWS, LANE), 1) >= COLS
    for m in range(MEMBERS):
        cot_out_ref[m] = jnp.where(spare, cut, cots[:, m * LANE : (m + 1) * LANE]).astype(BF)
    spread_taps(dw_ref, wb_ref)
    transpose_maps(maps_ref, rows_ref, local_sems, xt_ref)
    greeted(weights.greetings())
    weights.start(wq_ref)
    members_start(cot_out_ref, cot_in_ref, member_sems, 0)

    @pl.loop(0, CHUNKS)
    def _(chunk):
        conv_chunk(chunk, xt_ref, xp_ref, yp_ref, wb_ref, bias_ref, cv_ref)

    total = normalise(cv_ref, inv_ref, (0, SIDE), jnp.zeros((ROWS, C), F32))
    gain = gain_ref[...].reshape(1, C)
    pooled = (total * gain * (1.0 / AREA)).astype(BF)
    win_copy.wait()
    embed = dot(pooled, win_ref[...]).astype(BF)

    select, slots = send_rows(slot_ref)
    packed = jnp.concatenate([spread(embed), slots], axis=0)
    out_ref[...] = dot(select, packed).astype(BF).reshape(SLIDES, PACK, LANE)
    exchange_start(out_ref, in_ref, route_sems.at[0], route_sems.at[1])
    weights.hand_on()
    spread_slots, mask = slot_spread(), head_mask()
    members_wait(cot_in_ref, member_sems, 0)
    upstream = cot_in_ref[...].reshape(WIDE, LANE)
    cut = upstream[:, COLS : COLS + 1].astype(F32).astype(jnp.int32)
    allowed = allowed_pairs(member, seg_ref, dil_ref, cut)
    exchange_wait(out_ref, in_ref, route_sems.at[0], route_sems.at[1])
    arrived = in_ref[...].reshape(SLIDES * PACK, LANE)
    place = place_rows(spread_slots, arrived)
    blocks_ref[member] = gather_chunks(dot_first(place, arrived).astype(BF))
    members_start(None, blocks_ref, member_sems, 1, True)
    weights.finish()
    members_wait(blocks_ref, member_sems, 1)
    mixed, partial = attention(
        blocks_ref[...].reshape(WIDE, C), upstream[:, :COLS], w3_ref, mask, allowed)
    part_out_ref[...] = partial.astype(BF).reshape(MEMBERS, ROWS, C)
    members_start(part_out_ref, part_in_ref, member_sems, 2)
    padded = jnp.concatenate([mixed, jnp.zeros((WIDE, LANE - COLS), F32)], axis=1)
    mixed_out_ref[...] = padded.astype(BF).reshape(MEMBERS, ROWS, LANE)
    members_start(mixed_out_ref, mixed_in_ref, member_sems, 3)
    members_wait(part_in_ref, member_sems, 2)
    dblock = jnp.sum(part_in_ref[...].astype(F32), axis=0).astype(BF)
    back_out_ref[...] = dot(place, spread(dblock)).astype(BF).reshape(SLIDES, PACK, LANE)
    exchange_start(back_out_ref, back_in_ref, route_sems.at[2], route_sems.at[3])
    members_wait(mixed_in_ref, member_sems, 3)
    every = jnp.concatenate([mixed_in_ref[m] for m in range(MEMBERS)], axis=1)
    attn_ref[...] = dot_last(every, pick_ref[...]).astype(BF)
    weights.end()
    exchange_wait(back_out_ref, back_in_ref, route_sems.at[2], route_sems.at[3])
    returned = back_in_ref[...].reshape(SLIDES * PACK, LANE)
    dembed = gather_chunks(dot_first(select[:, : CHUNKS * ROWS], returned).astype(BF))
    dpool = dot_last(dembed, win_ref[...])

    bias_grad = conv_grads(dpool, gain, cv_ref, inv_ref)
    norm_ref[0:1] = jnp.sum(bias_grad, axis=0, keepdims=True)
    norm_ref[1:2] = jnp.sum(dpool * total, axis=0, keepdims=True) * (1.0 / AREA)
    sp_ref[...] = jnp.zeros(sp_ref.shape, F32)

    @pl.loop(0, CHUNKS)
    def _(chunk):
        lanes = pl.ds(pl.multiple_of(chunk * LANE, LANE), LANE)
        blocks = tap_grads(chunk, xp_ref, yp_ref, cv_ref, sp_ref)
        last = iota((8, LANE), 0) == TAPS
        for k in range(2):
            blocks[k] = jnp.where(last, norm_ref[k : k + 1, lanes], blocks[k])
        blocks.append(jnp.zeros((8, LANE), F32))
        flat_ref[:, lanes] = jnp.concatenate(blocks, axis=0).astype(BF)
        send_chunk(chunk, flat_ref, near_ref, sum_sems)

    reduce_all(flat_ref, near_ref, far_ref, res_ref, far_out_ref, sum_sems)
    sums_ref[...] = res_ref[...]


def finish_kernel(attn_ref, res_ref, out_ref, kernel_ref, norm_ref):
    out_ref[...] = attn_ref[...]
    result = res_ref[...].astype(F32)
    for r in range(TAPS):
        for s in range(TAPS):
            kernel_ref[r * TAPS + s : r * TAPS + s + 1] = result[s * 8 + r : s * 8 + r + 1]
    for k in range(2):
        norm_ref[k : k + 1] = result[k * 8 + TAPS : k * 8 + TAPS + 1]


VMEM_LIMIT = 60 * 1024 * 1024


def params(**extra):
    return pltpu.CompilerParams(vmem_limit_bytes=VMEM_LIMIT, **extra)


def vmem(count):
    return [pl.BlockSpec(memory_space=pltpu.VMEM)] * count


def smem(count):
    return [pl.BlockSpec(memory_space=pltpu.SMEM)] * count


def shape(*dims, kind=BF):
    return jax.ShapeDtypeStruct(dims, kind)


def body(
    tile_maps, dw_kernel, conv_bias, norm_gain, w_in, w_qkv, seg_len, dilation,
    tile_slot, slide_lengths, cotangent,
):
    dma = pltpu.SemaphoreType.DMA
    hbm = [pl.BlockSpec(memory_space=pl.ANY)]
    message = pltpu.VMEM((SLIDES, PACK, LANE), BF)
    wide = pltpu.VMEM((MEMBERS, ROWS, C), BF)
    narrow = pltpu.VMEM((MEMBERS, ROWS, LANE), BF)
    attn, sums = pl.pallas_call(
        step_kernel,
        out_shape=[shape(ROWS, C), shape(SUM_ROWS, C)],
        in_specs=hbm + vmem(3) + hbm + vmem(1) + smem(4) + vmem(1),
        out_specs=vmem(2),
        scratch_shapes=[
            pltpu.VMEM((SIDE, ROWS, SIDE, C), BF), pltpu.VMEM((SIDE, SIDE, ROWS, C), F32),
            pltpu.VMEM((AREA, ROWS, C), F32), pltpu.VMEM((AREA, ROWS, LANE), F32),
            pltpu.VMEM((POINTS, TAPS, 8, C), F32), pltpu.VMEM((C, C), BF),
            pltpu.VMEM((3, SHARE, HEAD, C), BF), pltpu.VMEM((3, 16, C), BF), message, message, message, message,
            pltpu.VMEM((C, MEMBERS * LANE), BF), narrow, narrow, wide, wide, wide, narrow, narrow,
            pltpu.VMEM((POINTS, SIDE, ROWS, C), F32), pltpu.VMEM((POINTS, SIDE, ROWS, LANE), F32),
            pltpu.VMEM((POINTS, 8, LANE), F32), pltpu.VMEM((2, C), F32), pltpu.VMEM((SUM_ROWS, C), BF),
            pltpu.VMEM((PLANE, 16, LANE), BF), pltpu.VMEM((SLIDES, 16, LANE), BF),
            pltpu.VMEM((2, 16, LANE), BF), pltpu.VMEM((SUM_ROWS, C), BF),
            dma((9,)), dma((2,)), dma((2,)), dma((7,)), dma((2, 4)), dma((4,)), dma((6,)),
        ],
        compiler_params=params(collective_id=1, has_side_effects=True),
    )(
        tile_maps, dw_kernel, conv_bias, norm_gain, w_in, w_qkv.T,
        seg_len, dilation, tile_slot, slide_lengths, cotangent,
    )
    return pl.pallas_call(
        finish_kernel,
        out_shape=[shape(ROWS, C), shape(49, C, kind=F32), shape(2, C, kind=F32)],
        in_specs=vmem(2),
        out_specs=vmem(3),
    )(attn, sums)


def solution(mesh):
    both = ("tile", "slide")
    in_specs = (
        P(both, None, None, None), P(), P(), P(), P(), P(None, "slide"), P(), P(),
        P(both), P(both, None), P(both, None),
    )
    out_specs = (P(both, None), P(), P())
    return jax.shard_map(body, mesh=mesh, in_specs=in_specs, out_specs=out_specs, check_vma=False)
```
